256 devices in a mesh: lat: 4 (over x_hi, core), lon: 64 (over z, y, x_lo).
Axes of the slice: x: 4 (x_hi: 2, x_lo: 2; x = x_hi * 2 + x_lo), y: 4, z: 8, core: 2. Of those that a mesh axis runs over, the one named last changes fastest.
Arguments:
- tokens: bfloat16 [2, 24, 768, 1024], P(None, 'lat', 'lon'), may hold values from -6 to 6
- cotangent: bfloat16 [2, 24, 768, 1024], P(None, 'lat', 'lon'), may hold values from -16 to 16
- qkv_weight: bfloat16 [1024, 3072], replicated, may hold values from -0.1875 to 0.1875
- out_weight: bfloat16 [1024, 1024], replicated, may hold values from -0.1875 to 0.1875
- bias_table: float32 [759, 16], replicated, may hold values from -12 to 332
- rel_index: int32 [144, 144], replicated, may hold values from 0 to 758
Outputs:
- token_grad: bfloat16 [2, 24, 768, 1024], P(None, 'lat', 'lon')
- out_grad: float32 [1024, 1024], P('lat', 'lon')
- table_grad: float32 [759, 16], replicated
The draws below stay inside these ranges and needn't reach their ends.
All inputs are finite; a program needn't handle non-finite values.
Results may differ from the reference program's by a relative error of at most 0.013.
Values may be sent and summed in bfloat16 or wider, within the bound.
No kernel may reach another device: no remote copies, remote signals or barrier semaphores. Data moves between devices by JAX's collectives and lax.ppermute only.
A program may use at most 128 MiB of HBM per device.

```python
import jax
import jax.numpy as jnp
from jax import lax

D = 1024
HEADS = 16
LEVELS = 2
WLAT = 6
WLON = 12
LAT_DEV = 6
LON_DEV = 12
LAT = 24
LON = 768
WIN = 144
NREL = 759


def draw_bias_table(key, part):
    key = jax.random.fold_in(key, 7)
    base_key = jax.random.fold_in(key, 0)
    base = jnp.clip(jax.random.normal(base_key, (NREL, HEADS), jnp.float32), -6.0, 6.0)
    return base


def place_ends(values, rng, smallest, largest):
    index_at = [jax.random.randint(jax.random.fold_in(rng, axis), (), 0, length) for axis, length in enumerate(values.shape)]
    main_axis = values.shape.index(max(values.shape))
    beside = index_at[:main_axis] + [(index_at[main_axis] + 1) % values.shape[main_axis]] + index_at[main_axis + 1:]
    return values.at[tuple(index_at)].set(smallest).at[tuple(beside)].set(largest)


def strengthened(values, rng, source, target, parts, factor):
    def block_of(axis_at):
        return (jnp.arange(values.shape[axis_at]) // (values.shape[axis_at] // parts)).reshape((-1,) + (1,) * (values.ndim - 1 - axis_at))

    one_side = jax.random.permutation(rng, parts)[block_of(target)]
    other_side = (block_of(target) + parts // 2) % parts
    return jnp.where((block_of(source) == one_side) | (block_of(source) == other_side), factor * values, values)


def shard_levels(key, dims, cuts, least, largest):
    gain, own = 1.0, jax.random.fold_in(key, 6)
    for position, parts in cuts:
        draws = jnp.exp(jax.random.uniform(jax.random.fold_in(own, position), (parts,), jnp.float32, least / len(cuts), largest / len(cuts)))
        gain = gain * jnp.repeat(draws, dims[position] // parts).reshape([-1 if axis == position else 1 for axis in range(len(dims))])
    return gain


def gaussian(stream_key, shape, deviation, most, shards=(), held_as=jnp.bfloat16):
    level = shard_levels(stream_key, shape, shards, -0.22, 0.18) if shards else 1.0
    result = jax.random.normal(stream_key, shape, jnp.float32) * deviation * level
    return jnp.minimum(jnp.maximum(result, -most), most).astype(held_as)


def bell_draw_with(rng, extent, deviation, bound, cuts, heavy, kind=jnp.bfloat16):
    values = deviation * jax.random.normal(rng, extent, jnp.float32)
    if cuts:
        values = values * shard_levels(rng, extent, cuts, -0.22, 0.18)
    return jnp.clip(strengthened(values, jax.random.fold_in(rng, 3), *heavy), -bound, bound).astype(kind)


def setup_inputs(seed: int = 0) -> dict:
    arg_keys = jax.random.split(jax.random.key(seed), 7)
    return {
        "tokens": gaussian(arg_keys[0], (LEVELS, LAT, LON, D), 1.0, 6.0, ((1, 4), (2, 64))),
        "cotangent": bell_draw_with(arg_keys[1], (LEVELS, LAT, LON, D), 1.0, 16.0, ((1, 4), (2, 64)), (2, 3, 64, 4.0)),
        "qkv_weight": gaussian(arg_keys[2], (D, 3 * D), D ** -0.5, 0.1875),
        "out_weight": gaussian(arg_keys[3], (D, D), D ** -0.5, 0.1875),
        "bias_table": draw_bias_table(jax.random.fold_in(arg_keys[6], 71), 0),
        "rel_index": place_ends(jax.random.randint(arg_keys[5], (WIN, WIN), 0, NREL), jax.random.fold_in(arg_keys[5], 1), 0, NREL - 1).astype(jnp.int32),
    }


def to_windows(field_block, lat_win, lon_win):
    level_count = field_block.shape[0]
    lat_rows = field_block.shape[1]
    lon_cols = field_block.shape[2]
    trailing = field_block.shape[3:]
    shaped = field_block.reshape((level_count, lat_rows // lat_win, lat_win, lon_cols // lon_win, lon_win) + trailing)
    order_axes = (1, 3, 0, 2, 4) + tuple(range(5, 5 + len(trailing)))
    return shaped.transpose(order_axes).reshape((-1, level_count * lat_win * lon_win) + trailing)

def from_windows(windows, level_count, lat_rows, lon_cols, lat_win, lon_win):
    features = windows.shape[-1]
    shaped = windows.reshape(lat_rows // lat_win, lon_cols // lon_win, level_count, lat_win, lon_win, features)
    return shaped.transpose(2, 0, 3, 1, 4, 5).reshape(level_count, lat_rows, lon_cols, features)

def half_again(values):
    return lax.optimization_barrier(values.astype(jnp.bfloat16)).astype(jnp.float32)

def window_pass(tok_win, cot_win, allowed, bias, qkv_weight, out_weight):
    win_tokens, features = tok_win.shape
    head_count = bias.shape[0]
    head_size = features // head_count
    scaling = head_size ** (-0.5)
    as_float = tok_win.astype(jnp.float32)
    centred = as_float - lax.optimization_barrier(jnp.mean(as_float, axis=1, keepdims=True))
    inv_std = lax.rsqrt(lax.optimization_barrier(jnp.mean(centred * centred, axis=1, keepdims=True)) + 1e-05)
    normed = centred * inv_std
    hidden = normed.astype(jnp.bfloat16)
    projected = jnp.dot(hidden, qkv_weight, preferred_element_type=jnp.float32).astype(jnp.bfloat16)

    def split_heads(values):
        return values.reshape(win_tokens, head_count, head_size).astype(jnp.float32)
    query_heads = split_heads(projected[:, :features])
    key_heads = split_heads(projected[:, features:2 * features])
    value_heads = split_heads(projected[:, 2 * features:])
    scores = jnp.einsum('ihd,jhd->hij', query_heads, key_heads) * scaling + bias
    scores = jnp.where(allowed[None], scores, -jnp.inf)
    row_max = lax.optimization_barrier(jnp.max(scores, axis=2, keepdims=True))
    expo = jnp.exp(scores - row_max)
    probs = expo / lax.optimization_barrier(jnp.sum(expo, axis=2, keepdims=True))
    probs_half = half_again(probs)
    attended = jnp.einsum('hij,jhd->ihd', probs_half, value_heads).astype(jnp.bfloat16).reshape(win_tokens, features)
    grad_att = jnp.dot(cot_win, out_weight.T, preferred_element_type=jnp.float32).astype(jnp.bfloat16)
    grad_heads = split_heads(grad_att)
    grad_probs = jnp.einsum('ihd,jhd->hij', grad_heads, value_heads)
    grad_values = jnp.einsum('hij,ihd->jhd', probs_half, grad_heads).astype(jnp.bfloat16)
    grad_scores = probs * (grad_probs - lax.optimization_barrier(jnp.sum(probs * grad_probs, axis=2, keepdims=True)))
    scaled_half = half_again(grad_scores * scaling)
    grad_query = jnp.einsum('hij,jhd->ihd', scaled_half, key_heads).astype(jnp.bfloat16)
    grad_key = jnp.einsum('hij,ihd->jhd', scaled_half, query_heads).astype(jnp.bfloat16)
    stacked = jnp.concatenate([grad_query.reshape(win_tokens, features), grad_key.reshape(win_tokens, features), grad_values.reshape(win_tokens, features)], axis=1)
    grad_normed = jnp.dot(stacked, qkv_weight.T, preferred_element_type=jnp.float32)
    branch = (grad_normed - lax.optimization_barrier(jnp.mean(grad_normed, axis=1, keepdims=True)) - normed * lax.optimization_barrier(jnp.mean(grad_normed * normed, axis=1, keepdims=True))) * inv_std
    grad_tok = (cot_win.astype(jnp.float32) + branch).astype(jnp.bfloat16)
    return (grad_tok, attended, grad_scores)

def reference(tokens, cotangent, qkv_weight, out_weight, bias_table, rel_index):
    level_count, lat_rows, lon_cols, features = tokens.shape
    half_lat = WLAT // 2
    half_lon = WLON // 2
    moved_tokens = jnp.roll(tokens, (-half_lat, -half_lon), axis=(1, 2))
    moved_cot = jnp.roll(cotangent, (-half_lat, -half_lon), axis=(1, 2))
    row_ids = jnp.arange(lat_rows, dtype=jnp.int32)
    wrapped = (row_ids >= lat_rows - half_lat).astype(jnp.int32)
    wrapped = jnp.broadcast_to(wrapped[None, :, None], (level_count, lat_rows, lon_cols))
    per_device = LAT_DEV // WLAT * (LON_DEV // WLON)
    win_tokens = level_count * WLAT * WLON
    tok_windows = to_windows(moved_tokens, WLAT, WLON).reshape(-1, per_device, win_tokens, features)
    cot_windows = to_windows(moved_cot, WLAT, WLON).reshape(-1, per_device, win_tokens, features)
    wrap_windows = to_windows(wrapped, WLAT, WLON).reshape(-1, per_device, win_tokens)
    bias = jnp.transpose(bias_table[rel_index], (2, 0, 1))
    head_count = bias.shape[0]

    def window_step(carry_state, inputs):
        weight_acc, score_acc = carry_state
        tok_part, cot_part, wrap_part = inputs
        allowed = wrap_part[:, :, None] == wrap_part[:, None, :]
        grad_tok, attended, grad_scores = jax.vmap(window_pass, in_axes=(0, 0, 0, None, None, None))(tok_part, cot_part, allowed, bias, qkv_weight, out_weight)
        weight_acc = weight_acc + jnp.dot(attended.reshape(-1, features).T, cot_part.reshape(-1, features), preferred_element_type=jnp.float32)
        score_acc = score_acc + lax.optimization_barrier(jnp.sum(grad_scores, axis=0))
        return ((weight_acc, score_acc), grad_tok)
    initial = (jnp.zeros((features, features), jnp.float32), jnp.zeros((head_count, win_tokens, win_tokens), jnp.float32))
    (out_grad, score_sum), grad_windows = lax.scan(window_step, initial, (tok_windows, cot_windows, wrap_windows))
    grad_moved = from_windows(grad_windows.reshape(-1, win_tokens, features), level_count, lat_rows, lon_cols, WLAT, WLON)
    token_grad = jnp.roll(grad_moved, (half_lat, half_lon), axis=(1, 2))
    table_grad = jax.ops.segment_sum(jnp.transpose(score_sum, (1, 2, 0)).reshape(-1, head_count), rel_index.reshape(-1), num_segments=bias_table.shape[0])
    return (token_grad, out_grad, table_grad)
```

```python
import functools

import jax
import jax.numpy as jnp
from jax import lax
from jax.experimental import pallas as pl
from jax.experimental.pallas import tpu as pltpu
from jax.sharding import Mesh
from jax.sharding import PartitionSpec as P

LEVELS = 2
WLAT = 6
WLON = 12
HALF_LAT = WLAT // 2
HALF_LON = WLON // 2
WIN = LEVELS * WLAT * WLON
PIECE = WIN // 4
HEADS = 16
HEAD = 64
D = HEADS * HEAD
NREL = 759
ROWS = 768
SCALE = HEAD ** (-0.5)
BF = jnp.bfloat16
F32 = jnp.float32
VMEM = pl.BlockSpec(memory_space=pltpu.VMEM)
ANY = pl.BlockSpec(memory_space=pl.ANY)
SMEM = pl.BlockSpec(memory_space=pltpu.SMEM)
LAT = ("xh", "core")
LON = ("z", "y", "xl")
NEAR = ("core", "y", "xl")
FAR = ("xh", "z")
ALL = ("xh", "core", "z", "y", "xl")

NT = (((1,), (1,)), ((), ()))
TN = (((0,), (0,)), ((), ()))


def dot(a, b, dims=(((1,), (0,)), ((), ()))):
    return lax.dot_general(a, b, dims, preferred_element_type=F32)


def params(mib):
    return pltpu.CompilerParams(vmem_limit_bytes=mib * 1024 * 1024)


def cost(flops, moved):
    return pl.CostEstimate(flops=flops, bytes_accessed=moved, transcendentals=0)


def groups():
    for level in range(LEVELS):
        for row in range(HALF_LAT):
            yield level, row, (level * HALF_LAT + row) * HALF_LON


def pack_kernel(tok, cot, lon_o, lat_o, dia_o, lon_s, lat_s, dia_s):
    for half, src in enumerate((tok, cot)):
        for level, row, at in groups():
            at = half * PIECE + at
            low = src[level, row].astype(F32)
            high = src[level, row + HALF_LAT].astype(F32)
            lon_s[at : at + HALF_LON] = high[:HALF_LON]
            dia_s[at : at + HALF_LON] = low[:HALF_LON]
            lat_s[at : at + HALF_LON] = low[HALF_LON:]
    lon_o[...] = lon_s[...].astype(BF)
    lat_o[...] = lat_s[...].astype(BF)
    dia_o[...] = dia_s[...].astype(BF)


def pack(tokens, cotangent):
    out = jax.ShapeDtypeStruct((2 * PIECE, D), BF)
    return pl.pallas_call(
        pack_kernel,
        out_shape=(out, out, out),
        in_specs=[VMEM, VMEM],
        out_specs=(VMEM, VMEM, VMEM),
        scratch_shapes=[pltpu.VMEM((2 * PIECE, D), F32)] * 3,
        compiler_params=params(16),
        name="pack",
    )(tokens, cotangent)


def bias_kernel(last, table, rel, out):
    row = lax.broadcasted_iota(jnp.int32, (WIN, 256), 0)
    col = lax.broadcasted_iota(jnp.int32, (WIN, 256), 1)
    half = WIN // 2
    split = (lax.rem(row, half) >= half // 2) == (lax.rem(col, half) >= half // 2)
    allowed = jnp.logical_or(split, last[0] == 0)
    index = rel[...]
    low = index & 127
    high = index >> 7

    def one_head(head, carry):
        line = table[pl.ds(head, 1), :]
        halves = []
        for side in (0, 1):
            lanes = slice(side * 128, side * 128 + 128)
            total = jnp.zeros((WIN, 128), F32)
            for part in range(ROWS // 128):
                source = jnp.broadcast_to(line[:, part * 128 : part * 128 + 128], (WIN, 128))
                found = jnp.take_along_axis(
                    source, low[:, lanes], axis=1, mode="promise_in_bounds"
                )
                total = jnp.where(high[:, lanes] == part, found, total)
            halves.append(jnp.where(allowed[:, lanes], total, -jnp.inf))
        out[head, :, :128] = halves[0]
        out[head, :, 128:] = halves[1][:, : WIN - 128]
        return carry

    lax.fori_loop(0, HEADS, one_head, 0)


def bias_of(last, table, rel):
    return pl.pallas_call(
        bias_kernel,
        out_shape=jax.ShapeDtypeStruct((HEADS, WIN, WIN), F32),
        in_specs=[SMEM, VMEM, VMEM],
        out_specs=VMEM,
        compiler_params=params(16),
        cost_estimate=cost(10_000_000, 4_000_000),
        name="bias",
    )(last, table, rel)


def gather_window(out, own, lon, lat, dia, offset):
    for level, row, at in groups():
        at = at + offset
        base = level * WLAT * WLON + row * WLON
        out[base : base + HALF_LON] = own[level, row + HALF_LAT].astype(F32)[HALF_LON:]
        out[base + HALF_LON : base + WLON] = lon[at : at + HALF_LON]
        base = base + HALF_LAT * WLON
        out[base : base + HALF_LON] = lat[at : at + HALF_LON]
        out[base + HALF_LON : base + WLON] = dia[at : at + HALF_LON]


def forward_kernel(
    tok, cot, lon, lat, dia, bias, wqkv_hbm, wout_hbm,
    cot_o, att_o, proj_o, gatt_o, ph_o, ds_o, g_o, normed_o, std_o,
    x_s, c_s, lon_s, lat_s, dia_s, wqkv, wout, sems,
):
    copies = [pltpu.make_async_copy(wout_hbm, wout, sems.at[3])]
    copies += [
        pltpu.make_async_copy(
            wqkv_hbm.at[:, pl.ds(part * D, D)], wqkv.at[part], sems.at[part]
        )
        for part in range(3)
    ]
    for copy in copies:
        copy.start()
    lon_s[...] = lon[...].astype(F32)
    lat_s[...] = lat[...].astype(F32)
    dia_s[...] = dia[...].astype(F32)
    gather_window(c_s, cot, lon_s, lat_s, dia_s, PIECE)
    gather_window(x_s, tok, lon_s, lat_s, dia_s, 0)
    cot_flat = c_s[...].astype(BF)
    cot_o[...] = cot_flat
    copies[0].wait()
    gatt_o[...] = dot(cot_flat, wout[...], NT).astype(BF)
    x = x_s[...]
    centred = x - jnp.mean(x, axis=1, keepdims=True)
    inv_std = lax.rsqrt(jnp.mean(centred * centred, axis=1, keepdims=True) + 1e-05)
    normed = centred * inv_std
    normed_o[...] = normed
    std_o[...] = jnp.broadcast_to(inv_std, (WIN, 128))
    hidden = normed.astype(BF)
    for part in range(3):
        copies[1 + part].wait()
        proj_o[part] = dot(hidden, wqkv[part]).astype(BF)
    lane = lax.broadcasted_iota(jnp.int32, (WIN, 128), 1)
    masks = (lane < HEAD, lane >= HEAD)
    zero = jnp.zeros((WIN, 128), BF)

    for pair in range(HEADS // 2):
        lanes = slice(pair * 128, pair * 128 + 128)
        query = proj_o[0, :, lanes]
        key = proj_o[1, :, lanes]
        value = proj_o[2, :, lanes]
        grad = gatt_o[:, lanes]
        attended = []
        for side in (0, 1):
            head = pair * 2 + side
            scores = dot(jnp.where(masks[side], query, zero), key, NT) * SCALE + bias[head]
            expo = jnp.exp(scores - jnp.max(scores, axis=1, keepdims=True))
            probs = expo * (1.0 / jnp.sum(expo, axis=1, keepdims=True))
            half = probs.astype(BF)
            ph_o[head] = half
            attended.append(dot(half, value))
            grad_probs = dot(jnp.where(masks[side], grad, zero), value, NT)
            inner = jnp.sum(probs * grad_probs, axis=1, keepdims=True)
            grad_scores = probs * (grad_probs - inner)
            g_o[head] = grad_scores
            ds_o[head] = (grad_scores * SCALE).astype(BF)
        block, core = pair // 4, (pair // 2) % 2
        at = block * 256 + (pair % 2) * 128
        att_o[core, :, at : at + 128] = jnp.where(masks[0], attended[0], attended[1]).astype(BF)


def forward(tokens, cotangent, lon, lat, dia, bias, qkv_weight, out_weight):
    square = (HEADS, WIN, WIN)
    return pl.pallas_call(
        forward_kernel,
        out_shape=(
            jax.ShapeDtypeStruct((WIN, D), BF),
            jax.ShapeDtypeStruct((2, WIN, D // 2), BF),
            jax.ShapeDtypeStruct((3, WIN, D), BF),
            jax.ShapeDtypeStruct((WIN, D), BF),
            jax.ShapeDtypeStruct(square, BF),
            jax.ShapeDtypeStruct(square, BF),
            jax.ShapeDtypeStruct(square, F32),
            jax.ShapeDtypeStruct((WIN, D), F32),
            jax.ShapeDtypeStruct((WIN, 128), F32),
        ),
        in_specs=[VMEM] * 6 + [ANY] * 2,
        out_specs=(VMEM,) * 9,
        scratch_shapes=[
            pltpu.VMEM((WIN, D), F32),
            pltpu.VMEM((WIN, D), F32),
            pltpu.VMEM((2 * PIECE, D), F32),
            pltpu.VMEM((2 * PIECE, D), F32),
            pltpu.VMEM((2 * PIECE, D), F32),
            pltpu.VMEM((3, D, D), BF),
            pltpu.VMEM((D, D), BF),
            pltpu.SemaphoreType.DMA((4,)),
        ],
        compiler_params=params(40),
        cost_estimate=cost(3_000_000_000, 24_000_000),
        name="forward",
    )(tokens, cotangent, lon, lat, dia, bias, qkv_weight, out_weight)


def table_kernel(grads, rel, out):
    blocks = ROWS // 256
    lane_id = lax.broadcasted_iota(jnp.int32, (256, WIN), 0)

    def one_row(i, total):
        index = rel[pl.ds(i, 1), :][:, :WIN]
        hot = jnp.where(lane_id == (index & 255), 1.0, 0.0).astype(BF)
        grad = grads[:, pl.ds(i, 1), :].reshape(HEADS, WIN)
        high = grad.astype(BF).astype(F32)
        both = jnp.concatenate([high, grad - high], axis=0)
        block = index >> 8
        picked = jnp.concatenate(
            [jnp.where(block == part, both, 0.0) for part in range(blocks)], axis=0
        ).astype(BF)
        return total + dot(picked, hot, NT)

    total = lax.fori_loop(
        0, WIN, one_row, jnp.zeros((blocks * 2 * HEADS, 256), F32), unroll=4
    )
    for part in range(blocks):
        at = part * 2 * HEADS
        out[part * HEADS : (part + 1) * HEADS] = (
            total[at : at + HEADS] + total[at + HEADS : at + 2 * HEADS]
        )


def table_of(grads, rel):
    return pl.pallas_call(
        table_kernel,
        out_shape=jax.ShapeDtypeStruct((ROWS // 256 * HEADS, 256), F32),
        in_specs=[VMEM, VMEM],
        out_specs=VMEM,
        compiler_params=params(24),
        cost_estimate=cost(3_000_000_000, 4_000_000),
        name="table",
    )(grads, rel)


def backward_kernel(
    ph, ds, proj, gatt, cot, normed, std, wqkv_hbm, own_o, lon_o, lat_o, dia_o,
    stacked, grad_s, piece_s, wqkv, sems,
):
    copies = [
        pltpu.make_async_copy(
            wqkv_hbm.at[:, pl.ds(part * D, D)], wqkv.at[part], sems.at[part]
        )
        for part in range(3)
    ]
    for copy in copies:
        copy.start()
    lane = lax.broadcasted_iota(jnp.int32, (WIN, 128), 1)
    first = lane < HEAD
    for pair in range(HEADS // 2):
        lanes = slice(pair * 128, pair * 128 + 128)
        query = proj[0, :, lanes]
        key = proj[1, :, lanes]
        grad = gatt[:, lanes]
        found = ([], [], [])
        for side in (0, 1):
            head = pair * 2 + side
            weights = ds[head]
            found[0].append(dot(weights, key))
            found[1].append(dot(weights, query, TN))
            found[2].append(dot(ph[head], grad, TN))
        for part in range(3):
            stacked[part, :, lanes] = jnp.where(first, *found[part]).astype(BF)
    total = jnp.zeros((WIN, D), F32)
    for part in range(3):
        copies[part].wait()
        total = total + dot(stacked[part], wqkv[part], NT)
    norm = normed[...]
    branch = (
        total
        - jnp.mean(total, axis=1, keepdims=True)
        - norm * jnp.mean(total * norm, axis=1, keepdims=True)
    ) * std[:, :1]
    grad_s[...] = cot[...].astype(F32) + branch
    for which, out in enumerate((own_o, lon_o, lat_o, dia_o)):
        shift = (which // 2) * HALF_LAT * WLON + (which % 2) * HALF_LON
        for level, row, at in groups():
            base = level * WLAT * WLON + row * WLON + shift
            piece_s[at : at + HALF_LON] = grad_s[base : base + HALF_LON]
        out[...] = piece_s[...].astype(BF)


def backward(ph, ds, proj, gatt, cot, normed, std, qkv_weight):
    piece = jax.ShapeDtypeStruct((PIECE, D), BF)
    return pl.pallas_call(
        backward_kernel,
        out_shape=(piece,) * 4,
        in_specs=[VMEM] * 7 + [ANY],
        out_specs=(VMEM,) * 4,
        scratch_shapes=[
            pltpu.VMEM((3, WIN, D), BF),
            pltpu.VMEM((WIN, D), F32),
            pltpu.VMEM((PIECE, D), F32),
            pltpu.VMEM((3, D, D), BF),
            pltpu.SemaphoreType.DMA((3,)),
        ],
        compiler_params=params(32),
        cost_estimate=cost(2_000_000_000, 16_000_000),
        name="backward",
    )(ph, ds, proj, gatt, cot, normed, std, qkv_weight)


def join_kernel(own, lon, lat, dia, out, own_s, lon_s, lat_s, dia_s, line):
    own_s[...] = own[...].astype(F32)
    lon_s[...] = lon[...].astype(F32)
    lat_s[...] = lat[...].astype(F32)
    dia_s[...] = dia[...].astype(F32)
    for level, row, at in groups():
        line[:HALF_LON] = dia_s[at : at + HALF_LON]
        line[HALF_LON:] = lat_s[at : at + HALF_LON]
        out[level, row] = line[...].astype(BF)
        line[:HALF_LON] = lon_s[at : at + HALF_LON]
        line[HALF_LON:] = own_s[at : at + HALF_LON]
        out[level, row + HALF_LAT] = line[...].astype(BF)


def join(own, lon, lat, dia):
    return pl.pallas_call(
        join_kernel,
        out_shape=jax.ShapeDtypeStruct((LEVELS, WLAT, WLON, D), BF),
        in_specs=[VMEM] * 4,
        out_specs=VMEM,
        scratch_shapes=[pltpu.VMEM((PIECE, D), F32)] * 4 + [pltpu.VMEM((WLON, D), F32)],
        compiler_params=params(16),
        name="join",
    )(own, lon, lat, dia)


def shift(array, axes, by):
    peers = lax.axis_size(axes)
    return lax.ppermute(array, axes, [(i, (i + by) % peers) for i in range(peers)])


def shift_both(array, by):
    lats, lons = lax.axis_size(LAT), lax.axis_size(LON)
    pairs = [
        (a * lons + b, ((a + by) % lats) * lons + (b + by) % lons)
        for a in range(lats)
        for b in range(lons)
    ]
    return lax.ppermute(array, ALL, pairs)


def pick(array, index, axis):
    return lax.dynamic_index_in_dim(array, index, axis, keepdims=False)


def shared_sum(array, axes):
    peers = lax.axis_size(axes)
    copies = jnp.broadcast_to(array[None], (peers,) + array.shape)
    return jnp.sum(lax.all_to_all(copies, axes, 0, 0, tiled=True), axis=0)


def reduce_out(cot, att):
    core = lax.axis_index("core")
    att_far = lax.ppermute(pick(att, 1 - core, 0), "core", [(0, 1), (1, 0)])
    cot_far = lax.ppermute(cot, "core", [(0, 1), (1, 0)])
    mine = jnp.concatenate([pick(att, core, 0), att_far], axis=0)
    partial = dot(jnp.concatenate([cot, cot_far], axis=0), mine, TN).astype(BF)

    zs, ys, xls, xhs = (lax.axis_size(name) for name in ("z", "y", "xl", "xh"))
    partial = partial.reshape(zs, ys, xls * 16, D // 2)
    me = lax.axis_index("y")
    total = pick(partial, me, 1).astype(F32)
    for by in range(1, ys):
        total = total + shift(pick(partial, (me + by) % ys, 1), "y", by).astype(F32)
    partial = total.astype(BF).reshape(zs, xls, 16, xhs, 256)

    xh, xl = lax.axis_index("xh"), lax.axis_index("xl")
    total = pick(pick(partial, xh, 3), xl, 1).astype(F32)
    for flip in range(1, 4):
        a, b = flip // 2, flip % 2
        piece = pick(pick(partial, xh ^ a, 3), xl ^ b, 1)
        pairs = [(i, i ^ flip) for i in range(4)]
        total = total + lax.ppermute(piece, ("xh", "xl"), pairs).astype(F32)
    partial = total.astype(BF)

    pieces = lax.all_to_all(partial, "z", 0, 0, tiled=True)
    return jnp.sum(pieces.astype(F32), axis=0).T


def body(tokens, cotangent, qkv_weight, out_weight, bias_table, rel_index):
    last = (lax.axis_index("xh") * 2 + lax.axis_index("core") == 3).astype(jnp.int32).reshape(1)
    send = pack(tokens, cotangent)
    lon = shift(send[0], LON, -1)
    lat = shift(send[1], LAT, -1)
    dia = shift_both(send[2], -1)
    table = jnp.pad(bias_table.T, ((0, 0), (0, ROWS - NREL)))
    rel = jnp.pad(rel_index, ((0, 0), (0, 256 - WIN)))
    bias = bias_of(last, table, rel)
    cot, att, proj, gatt, ph, ds, grads, normed, std = forward(
        tokens, cotangent, lon, lat, dia, bias, qkv_weight, out_weight
    )
    out_grad = reduce_out(cot, att)
    sums = table_of(grads, rel)
    sums = shared_sum(shared_sum(sums, NEAR), FAR)
    table_grad = sums.reshape(ROWS // 256, HEADS, 256).transpose(0, 2, 1).reshape(ROWS, HEADS)[:NREL]
    own, lon, lat, dia = backward(ph, ds, proj, gatt, cot, normed, std, qkv_weight)
    token_grad = join(own, shift(lon, LON, 1), shift(lat, LAT, 1), shift_both(dia, 1))
    return (token_grad, out_grad, table_grad)


def solution(mesh):
    fine = Mesh(mesh.devices.reshape(2, 2, 8, 4, 2), ALL)
    grid = P(None, LAT, LON, None)
    return jax.shard_map(
        body,
        mesh=fine,
        in_specs=(grid, grid, P(), P(), P(), P()),
        out_specs=(grid, P(LAT, LON), P()),
        check_vma=False,
    )
```

```python
import functools

import jax
import jax.numpy as jnp
from jax import lax
from jax.experimental import pallas as pl
from jax.experimental.pallas import tpu as pltpu
from jax.sharding import Mesh
from jax.sharding import PartitionSpec as P

LEVELS = 2
WLAT = 6
WLON = 12
HALF_LAT = WLAT // 2
HALF_LON = WLON // 2
WIN = LEVELS * WLAT * WLON
PIECE = WIN // 4
HEADS = 16
HEAD = 64
D = HEADS * HEAD
NREL = 759
ROWS = 768
PARTS = ROWS // 128
SIDE = 6
TAIL = WIN - 128
STACK = WIN // SIDE
ROWS_PACKED = WIN + STACK
SCALE = HEAD ** (-0.5)
BF = jnp.bfloat16
F32 = jnp.float32
VMEM = pl.BlockSpec(memory_space=pltpu.VMEM)
ANY = pl.BlockSpec(memory_space=pl.ANY)
SMEM = pl.BlockSpec(memory_space=pltpu.SMEM)
LAT = ("xh", "core")
LON = ("z", "y", "xl")
XS = ("xh", "xl")
ALL = ("xh", "core", "z", "y", "xl")

NT = (((1,), (1,)), ((), ()))
TN = (((0,), (0,)), ((), ()))


def dot(a, b, dims=(((1,), (0,)), ((), ()))):
    return lax.dot_general(a, b, dims, preferred_element_type=F32)


def params(mib):
    return pltpu.CompilerParams(vmem_limit_bytes=mib * 1024 * 1024)


def cost(flops, moved):
    return pl.CostEstimate(flops=flops, bytes_accessed=moved, transcendentals=0)


def groups():
    for level in range(LEVELS):
        for row in range(HALF_LAT):
            yield level, row, (level * HALF_LAT + row) * HALF_LON


def pack_kernel(tok, cot, lon_o, lat_o, dia_o, lon_s, lat_s, dia_s):
    for half, src in enumerate((tok, cot)):
        for level, row, at in groups():
            at = half * PIECE + at
            low = src[level, row].astype(F32)
            high = src[level, row + HALF_LAT].astype(F32)
            lon_s[at : at + HALF_LON] = high[:HALF_LON]
            dia_s[at : at + HALF_LON] = low[:HALF_LON]
            lat_s[at : at + HALF_LON] = low[HALF_LON:]
    lon_o[...] = lon_s[...].astype(BF)
    lat_o[...] = lat_s[...].astype(BF)
    dia_o[...] = dia_s[...].astype(BF)


def pack(tokens, cotangent):
    out = jax.ShapeDtypeStruct((2 * PIECE, D), BF)
    return pl.pallas_call(
        pack_kernel,
        out_shape=(out, out, out),
        in_specs=[VMEM, VMEM],
        out_specs=(VMEM, VMEM, VMEM),
        scratch_shapes=[pltpu.VMEM((2 * PIECE, D), F32)] * 3,
        compiler_params=params(4),
        cost_estimate=cost(1_000_000, 6_000_000),
        name="pack",
    )(tokens, cotangent)


def bias_kernel(last, table, rel, out, packed, table_s, rel_s, tail_s):
    table_s[:, :NREL] = table[...]
    rel_s[:, :TAIL] = rel[:, 128:]
    packed[:WIN] = rel[:, :128]
    lane = lax.broadcasted_iota(jnp.int32, (STACK, 128), 1)
    block = lane // TAIL
    tail = rel_s[:STACK]
    for side in range(1, SIDE):
        moved = pltpu.roll(rel_s[side * STACK : side * STACK + STACK], side * TAIL, 1)
        tail = jnp.where(block == side, moved, tail)
    packed[WIN:] = jnp.where(block < SIDE, tail, 0)
    free = last[0] == 0
    half = WIN // 2

    def wrapped(index):
        return lax.rem(index, half) >= half // 2

    row = lax.broadcasted_iota(jnp.int32, (8, 128), 0)
    col = lax.broadcasted_iota(jnp.int32, (8, 128), 1)

    def look_up(step):
        index = packed[pl.ds(pl.multiple_of(step * 8, 8), 8), :]
        low, high = index & 127, index >> 7
        masks = [high == part for part in range(PARTS)]
        for head in range(HEADS):
            total = jnp.zeros((8, 128), F32)
            for part in range(PARTS):
                line = table_s[head : head + 1, part * 128 : part * 128 + 128]
                source = jnp.broadcast_to(line, (8, 128))
                found = jnp.take_along_axis(source, low, axis=1, mode="promise_in_bounds")
                total = jnp.where(masks[part], found, total)
            yield head, total

    def main_rows(step, carry):
        allowed = jnp.logical_or(wrapped(row + step * 8) == wrapped(col), free)
        for head, total in look_up(step):
            out[head, pl.ds(pl.multiple_of(step * 8, 8), 8), :128] = jnp.where(
                allowed, total, -jnp.inf
            )
        return carry

    def tail_rows(step, carry):
        at = (step - WIN // 8) * 8
        allowed = jnp.logical_or(wrapped(col // TAIL * STACK + row + at), free)
        for head, total in look_up(step):
            tail_s[head, pl.ds(pl.multiple_of(at, 8), 8), :] = jnp.where(allowed, total, -jnp.inf)
        return carry

    lax.fori_loop(0, WIN // 8, main_rows, 0)
    lax.fori_loop(WIN // 8, ROWS_PACKED // 8, tail_rows, 0)
    for head in range(HEADS):
        found = tail_s[head]
        for side in range(SIDE):
            moved = found if side == 0 else pltpu.roll(found, 128 - side * TAIL, 1)
            out[head, side * STACK : side * STACK + STACK, 128:] = moved[:, :TAIL]


def bias_of(last, table, rel):
    return pl.pallas_call(
        bias_kernel,
        out_shape=(
            jax.ShapeDtypeStruct((HEADS, WIN, WIN), F32),
            jax.ShapeDtypeStruct((ROWS_PACKED, 128), jnp.int32),
        ),
        in_specs=[SMEM, VMEM, VMEM],
        out_specs=(VMEM, VMEM),
        scratch_shapes=[
            pltpu.VMEM((HEADS, ROWS), F32),
            pltpu.VMEM((WIN, 128), jnp.int32),
            pltpu.VMEM((HEADS, STACK, 128), F32),
        ],
        compiler_params=params(4),
        cost_estimate=cost(10_000_000, 28_000_000),
        name="bias",
    )(last, table, rel)


def gather_window(out, own, lon, lat, dia, offset):
    for level, row, at in groups():
        at = at + offset
        base = level * WLAT * WLON + row * WLON
        out[base : base + HALF_LON] = own[level, row + HALF_LAT].astype(F32)[HALF_LON:]
        out[base + HALF_LON : base + WLON] = lon[at : at + HALF_LON]
        base = base + HALF_LAT * WLON
        out[base : base + HALF_LON] = lat[at : at + HALF_LON]
        out[base + HALF_LON : base + WLON] = dia[at : at + HALF_LON]


def forward_kernel(
    tok, cot, lon, lat, dia, bias, wqkv_hbm,
    cot_o, att_o, proj, probs_o, normed_o, std_o,
    x_s, c_s, lon_s, lat_s, dia_s, wqkv, sems,
):
    copies = [
        pltpu.make_async_copy(
            wqkv_hbm.at[:, pl.ds(part * D, D)], wqkv.at[part], sems.at[part]
        )
        for part in range(3)
    ]
    for copy in copies:
        copy.start()
    lon_s[...] = lon[...].astype(F32)
    lat_s[...] = lat[...].astype(F32)
    dia_s[...] = dia[...].astype(F32)
    gather_window(x_s, tok, lon_s, lat_s, dia_s, 0)
    gather_window(c_s, cot, lon_s, lat_s, dia_s, PIECE)
    cot_o[...] = c_s[...].astype(BF)
    x = x_s[...]
    centred = x - jnp.mean(x, axis=1, keepdims=True)
    inv_std = lax.rsqrt(jnp.mean(centred * centred, axis=1, keepdims=True) + 1e-05)
    normed = centred * inv_std
    normed_o[...] = normed
    std_o[...] = jnp.broadcast_to(inv_std, (WIN, 128))
    hidden = normed.astype(BF)
    for part in range(3):
        copies[part].wait()
        proj[part] = dot(hidden, wqkv[part]).astype(BF)
    lane = lax.broadcasted_iota(jnp.int32, (WIN, 128), 1)
    masks = (lane < HEAD, lane >= HEAD)
    zero = jnp.zeros((WIN, 128), BF)

    for pair in range(HEADS // 2):
        lanes = slice(pair * 128, pair * 128 + 128)
        query = proj[0, :, lanes]
        key = proj[1, :, lanes]
        value = proj[2, :, lanes]
        attended = []
        for side in (0, 1):
            head = pair * 2 + side
            scores = dot(jnp.where(masks[side], query, zero), key, NT) * SCALE + bias[head]
            expo = jnp.exp(scores - jnp.max(scores, axis=1, keepdims=True))
            probs = expo * (1.0 / jnp.sum(expo, axis=1, keepdims=True))
            probs_o[head, :WIN] = probs[:, :128]
            probs_o[head, WIN:, : WIN - 128] = probs[:, 128:]
            attended.append(dot(probs.astype(BF), value))
        block, core = pair // 4, (pair // 2) % 2
        at = block * 256 + (pair % 2) * 128
        att_o[core, :, at : at + 128] = jnp.where(masks[0], attended[0], attended[1]).astype(BF)


def forward(tokens, cotangent, lon, lat, dia, bias, qkv_weight):
    return pl.pallas_call(
        forward_kernel,
        out_shape=(
            jax.ShapeDtypeStruct((WIN, D), BF),
            jax.ShapeDtypeStruct((2, WIN, D // 2), BF),
            jax.ShapeDtypeStruct((3, WIN, D), BF),
            jax.ShapeDtypeStruct((HEADS, 2 * WIN, 128), F32),
            jax.ShapeDtypeStruct((WIN, D), F32),
            jax.ShapeDtypeStruct((WIN, 128), F32),
        ),
        in_specs=[VMEM] * 6 + [ANY],
        out_specs=(VMEM,) * 6,
        scratch_shapes=[
            pltpu.VMEM((WIN, D), F32),
            pltpu.VMEM((WIN, D), F32),
            pltpu.VMEM((2 * PIECE, D), F32),
            pltpu.VMEM((2 * PIECE, D), F32),
            pltpu.VMEM((2 * PIECE, D), F32),
            pltpu.VMEM((3, D, D), BF),
            pltpu.SemaphoreType.DMA((3,)),
        ],
        compiler_params=params(44),
        cost_estimate=cost(1_000_000_000, 15_000_000),
        name="forward",
    )(tokens, cotangent, lon, lat, dia, bias, qkv_weight)


def backward_kernel(
    cot, std, wqkv, wout, probs, proj, normed, own_o, lon_o, lat_o, grads,
    gatt, stacked, grad_s, piece_s,
):
    gatt[...] = dot(cot[...], wout[...], NT).astype(BF)
    blank = jnp.zeros((WIN, 128 - TAIL), F32)
    lane = lax.broadcasted_iota(jnp.int32, (WIN, 128), 1)
    masks = (lane < HEAD, lane >= HEAD)
    zero = jnp.zeros((WIN, 128), BF)
    for pair in range(HEADS // 2):
        lanes = slice(pair * 128, pair * 128 + 128)
        query = proj[0, :, lanes]
        key = proj[1, :, lanes]
        value = proj[2, :, lanes]
        grad = gatt[:, lanes]
        found = ([], [], [])
        for side in (0, 1):
            head = pair * 2 + side
            prob = jnp.concatenate(
                [probs[head, :WIN], probs[head, WIN:, : WIN - 128]], axis=1
            )
            grad_probs = dot(jnp.where(masks[side], grad, zero), value, NT)
            inner = jnp.sum(prob * grad_probs, axis=1, keepdims=True)
            grad_scores = prob * (grad_probs - inner)
            grads[head, :WIN] = grad_scores[:, :128]
            tail = jnp.concatenate([grad_scores[:, 128:], blank], axis=1)
            packed = tail[:STACK]
            for at in range(1, SIDE):
                packed = packed + pltpu.roll(tail[at * STACK : at * STACK + STACK], at * TAIL, 1)
            grads[head, WIN:] = packed
            weights = (grad_scores * SCALE).astype(BF)
            found[0].append(dot(weights, key))
            found[1].append(dot(weights, query, TN))
            found[2].append(dot(prob.astype(BF), grad, TN))
        for part in range(3):
            stacked[part, :, lanes] = jnp.where(masks[0], *found[part]).astype(BF)
    total = jnp.zeros((WIN, D), F32)
    for part in range(3):
        total = total + dot(stacked[part], wqkv[:, part * D : part * D + D], NT)
    norm = normed[...]
    branch = (
        total
        - jnp.mean(total, axis=1, keepdims=True)
        - norm * jnp.mean(total * norm, axis=1, keepdims=True)
    ) * std[:, :1]
    grad_s[...] = cot[...].astype(F32) + branch
    for which in (0, 2, 1, 3):
        shift = (which // 2) * HALF_LAT * WLON + (which % 2) * HALF_LON
        for level, row, at in groups():
            base = level * WLAT * WLON + row * WLON + shift
            at = at + (PIECE if which == 3 else 0)
            piece_s[at : at + HALF_LON] = grad_s[base : base + HALF_LON]
        if which % 2 == 0:
            (own_o, lat_o)[which // 2][...] = piece_s[:PIECE].astype(BF)
    lon_o[...] = piece_s[...].astype(BF)


def backward(cot, std, qkv_weight, out_weight, probs, proj, normed):
    piece = jax.ShapeDtypeStruct((PIECE, D), BF)
    return pl.pallas_call(
        backward_kernel,
        out_shape=(
            piece,
            jax.ShapeDtypeStruct((2 * PIECE, D), BF),
            piece,
            jax.ShapeDtypeStruct((HEADS, ROWS_PACKED, 128), F32),
        ),
        in_specs=[VMEM] * 7,
        out_specs=(VMEM,) * 4,
        scratch_shapes=[
            pltpu.VMEM((WIN, D), BF),
            pltpu.VMEM((3, WIN, D), BF),
            pltpu.VMEM((WIN, D), F32),
            pltpu.VMEM((2 * PIECE, D), F32),
        ],
        compiler_params=params(8),
        cost_estimate=cost(2_000_000_000, 30_000_000),
        name="backward",
    )(cot, std, qkv_weight, out_weight, probs, proj, normed)


def table_kernel(grads, packed, after, out):
    lane_id = lax.broadcasted_iota(jnp.int32, (128, 128), 0)

    def two_rows(step, total):
        hots, grad_rows, blocks = [], [], []
        for which in (0, 1):
            row = step * 2 + which
            index = packed[pl.ds(row, 1), :]
            hots.append(jnp.where(lane_id == (index & 127), 1.0, 0.0).astype(BF))
            grad_rows.append(grads[pl.ds(row, HEADS, stride=ROWS_PACKED), :])
            blocks.append(index >> 7)
        grad = jnp.concatenate(grad_rows, axis=1)
        block = jnp.concatenate(blocks, axis=1)
        picked = jnp.concatenate(
            [jnp.where(block == part, grad, 0.0) for part in range(PARTS)], axis=0
        )
        return total + dot(picked.astype(BF), jnp.concatenate(hots, axis=1), NT)

    total = lax.fori_loop(
        0, ROWS_PACKED // 2, two_rows, jnp.zeros((PARTS * HEADS, 128), F32), unroll=4
    )
    total = total.astype(BF)
    for part in range(PARTS):
        at = part % 2 * 128
        out[part // 2, :, at : at + 128] = total[part * HEADS : part * HEADS + HEADS]


def table_of(grads, packed, after):
    return pl.pallas_call(
        table_kernel,
        out_shape=jax.ShapeDtypeStruct((PARTS // 2, HEADS, 256), BF),
        in_specs=[VMEM, VMEM, ANY],
        out_specs=VMEM,
        compiler_params=params(4),
        cost_estimate=cost(1_000, 1_000),
        name="table",
    )(grads.reshape(HEADS * ROWS_PACKED, 128), packed, after)


def by_y(place, total, outs):
    for step, out in enumerate(outs):
        out[...] = total[lax.rem(place[0] + step, len(outs))]


def outer_kernel(place, cot, cot_far, att, att_far, after, *refs):
    low_o, (keep, give, low_s, high_s) = refs[:4], refs[4:]
    total = dot(cot[...], att[0], TN) + dot(cot_far[...], att_far[0], TN)
    ys, depth = low_s.shape[:2]
    for xh in range(2):
        at = slice(xh * 128, xh * 128 + 128)
        low = total[:, xh * 256 : xh * 256 + 128].astype(BF).reshape(depth, ys, 32, 128)
        for y in range(ys):
            low_s[y, :, :, at] = low[:, y]
        high = total[:, xh * 256 + 128 : xh * 256 + 256].astype(BF).reshape(depth * ys, 2, 16, 128)
        for xl in range(2):
            high_s[xl, :, :, at] = high[:, xl]
    by_y(place, low_s, low_o)
    keep[...] = high_s[place[1]]
    give[...] = high_s[1 - place[1]]


def outer(place, depth, cot, cot_far, att, att_far, after):
    low, high = (depth, 32, 256), (depth * 4, 16, 256)
    return pl.pallas_call(
        outer_kernel,
        out_shape=(jax.ShapeDtypeStruct(low, BF),) * 4 + (jax.ShapeDtypeStruct(high, BF),) * 2,
        in_specs=[SMEM] + [VMEM] * 4 + [ANY],
        out_specs=(VMEM,) * 6,
        scratch_shapes=[pltpu.VMEM((4,) + low, BF), pltpu.VMEM((2,) + high, BF)],
        compiler_params=params(8),
        cost_estimate=cost(600_000_000, 3_000_000),
        name="outer",
    )(place, cot, cot_far, att, att_far, after)


def added(pieces):
    total = pieces[0][...].astype(F32)
    for piece in pieces[1:]:
        total = total + piece[...].astype(F32)
    return total


def turn_kernel(place, *refs):
    table = added(refs[6:8]).astype(BF)
    (keep, give), high_o, (low_s, high_s) = refs[9:11], refs[11:15], refs[15:]
    low = added(refs[:4]).astype(BF)
    for xl in range(2):
        low_s[xl] = low[:, xl * 16 : xl * 16 + 16]
    keep[...] = low_s[place[1]]
    give[...] = low_s[1 - place[1]]
    ys, depth = high_s.shape[:2]
    high = added(refs[4:6]).astype(BF).reshape((depth, ys) + high_s.shape[2:])
    for y in range(ys):
        high_s[y] = high[:, y]
    for step, out in enumerate(high_o):
        out[:depth] = high_s[lax.rem(place[0] + step, ys)]
        out[depth:] = table


def turn(place, low, high, tables, after):
    depth = low[0].shape[0]
    plain = jax.ShapeDtypeStruct((depth, 16, 256), BF)
    longer = jax.ShapeDtypeStruct((depth + PARTS // 2, 16, 256), BF)
    return pl.pallas_call(
        turn_kernel,
        out_shape=(plain,) * 2 + (longer,) * 4,
        in_specs=[SMEM] + [VMEM] * 8 + [ANY],
        out_specs=(VMEM,) * 6,
        scratch_shapes=[pltpu.VMEM((2,) + plain.shape, BF), pltpu.VMEM((4,) + plain.shape, BF)],
        compiler_params=params(4),
        name="turn",
    )(place, *low, *high, *tables, after)


def halve_kernel(place, *refs):
    keep, give, table_o, table_s = refs[6:]
    depth = keep.shape[0]
    upper = place[2] == 1
    for at, pieces in ((0, refs[:2]), (128, [ref.at[:depth] for ref in refs[2:6]])):
        total = added(pieces)
        near, far = total[:, :, :128], total[:, :, 128:]
        keep[:, :, at : at + 128] = jnp.where(upper, far, near).astype(BF)
        give[:depth, :, at : at + 128] = jnp.where(upper, near, far).astype(BF)
    for step in range(4):
        table_s[lax.rem(place[0] + 4 - step, 4)] = refs[2 + step][depth:]
    table = added([table_s.at[y] for y in range(4)]).astype(BF)
    give[depth:] = table
    table_o[...] = table


def halve(place, low, high):
    plain, longer = low[0].shape, high[0].shape
    table = (longer[0] - plain[0],) + plain[1:]
    return pl.pallas_call(
        halve_kernel,
        out_shape=(
            jax.ShapeDtypeStruct(plain, BF),
            jax.ShapeDtypeStruct(longer, BF),
            jax.ShapeDtypeStruct(table, BF),
        ),
        in_specs=[SMEM] + [VMEM] * 6,
        out_specs=(VMEM,) * 3,
        scratch_shapes=[pltpu.VMEM((4,) + table, BF)],
        compiler_params=params(4),
        name="halve",
    )(place, *low, *high)


def mix_kernel(place, keep, got, mine, beside, across, after, out, table_s):
    depth = keep.shape[0]
    at = place[2] * 2 + place[1]
    table_s[at] = mine[...]
    table_s[at ^ 1] = beside[...]
    table_s[at ^ 2] = got[depth:]
    table_s[at ^ 3] = across[...]
    table = added([table_s.at[x] for x in range(4)]).astype(BF)
    out[:, 0] = added((keep, got.at[:depth])).astype(BF)
    for z in range(depth):
        out[z, 1:] = table


def mix(place, keep, got, mine, beside, across, after):
    return pl.pallas_call(
        mix_kernel,
        out_shape=jax.ShapeDtypeStruct((keep.shape[0], 1 + PARTS // 2, 16, 256), BF),
        in_specs=[SMEM] + [VMEM] * 5 + [ANY],
        out_specs=VMEM,
        scratch_shapes=[pltpu.VMEM((4,) + mine.shape, BF)],
        compiler_params=params(4),
        name="mix",
    )(place, keep, got, mine, beside, across, after)


def final_kernel(pieces, out, table):
    total = added([pieces.at[z] for z in range(pieces.shape[0])])
    out[...] = total[0]
    for part in range(PARTS):
        at = part % 2 * 128
        lanes = min(128, NREL - part * 128)
        table[:, part * 128 : part * 128 + lanes] = total[1 + part // 2, :, at : at + lanes]


def final(pieces):
    return pl.pallas_call(
        final_kernel,
        out_shape=(
            jax.ShapeDtypeStruct((16, 256), F32),
            jax.ShapeDtypeStruct((HEADS, NREL), F32),
        ),
        in_specs=[VMEM],
        out_specs=(VMEM,) * 2,
        compiler_params=params(4),
        name="final",
    )(pieces)


def join_kernel(own, lon, lat, out, own_s, lon_s, lat_s, line):
    own_s[...] = own[...].astype(F32)
    lon_s[...] = lon[...].astype(F32)
    lat_s[...] = lat[...].astype(F32)
    for level, row, at in groups():
        line[:HALF_LON] = lat_s[at + PIECE : at + PIECE + HALF_LON]
        line[HALF_LON:] = lat_s[at : at + HALF_LON]
        out[level, row] = line[...].astype(BF)
        line[:HALF_LON] = lon_s[at : at + HALF_LON]
        line[HALF_LON:] = own_s[at : at + HALF_LON]
        out[level, row + HALF_LAT] = line[...].astype(BF)


def join(own, lon, lat):
    return pl.pallas_call(
        join_kernel,
        out_shape=jax.ShapeDtypeStruct((LEVELS, WLAT, WLON, D), BF),
        in_specs=[VMEM] * 3,
        out_specs=VMEM,
        scratch_shapes=[
            pltpu.VMEM((PIECE, D), F32),
            pltpu.VMEM((2 * PIECE, D), F32),
            pltpu.VMEM((2 * PIECE, D), F32),
            pltpu.VMEM((WLON, D), F32),
        ],
        compiler_params=params(4),
        name="join",
    )(own, lon, lat)


def shift(array, axes, by):
    peers = lax.axis_size(axes)
    return lax.ppermute(array, axes, [(i, (i + by) % peers) for i in range(peers)])


def shift_both(array, by):
    lats, lons = lax.axis_size(LAT), lax.axis_size(LON)
    pairs = [
        (a * lons + b, ((a + by) % lats) * lons + (b + by) % lons)
        for a in range(lats)
        for b in range(lons)
    ]
    return lax.ppermute(array, ALL, pairs)


def exchange(pieces, axes):
    return lax.all_to_all(pieces, axes, 0, 0, tiled=True)


def along_y(pieces):
    return [pieces[0]] + [shift(pieces[step], "y", step) for step in range(1, 4)]


def body(tokens, cotangent, qkv_weight, out_weight, bias_table, rel_index):
    places = {name: lax.axis_index(name).astype(jnp.int32) for name in ALL}
    core = places["core"]
    flat = jnp.stack([places["y"], places["xl"], places["xh"]])
    last = (places["xh"] * 2 + core == 3).astype(jnp.int32).reshape(1)
    swap = [(0, 1), (1, 0)]
    send = pack(tokens, cotangent)
    lon = shift(send[0], LON, -1)
    lat = shift(send[1], LAT, -1)
    dia = shift_both(send[2], -1)
    bias, packed = bias_of(last, bias_table.T, rel_index)
    cot, att, proj, probs, normed, std = forward(
        tokens, cotangent, lon, lat, dia, bias, qkv_weight
    )
    att_far = lax.ppermute(lax.dynamic_slice_in_dim(att, 1 - core, 1, 0), "core", swap)
    cot_far = lax.ppermute(cot, "core", swap)
    own, lon, lat, grads = backward(
        cot, std, qkv_weight, out_weight, probs, proj, normed
    )
    lon = shift(lon, LON, 1)
    att_own = lax.dynamic_slice_in_dim(att, core, 1, 0)
    pieces = outer(flat, lax.axis_size("z"), cot, cot_far, att_own, att_far, own)
    low, high = along_y(pieces[:4]), (pieces[4], lax.ppermute(pieces[5], "xl", swap))
    table = table_of(grads, packed, pieces[0])
    tables = (table, lax.ppermute(table, "core", swap))
    pieces = turn(flat, low, high, tables, lon)
    lat = shift(jnp.concatenate([lat, lon[PIECE:]], axis=0), LAT, 1)
    token_grad = join(own, lon, lat)
    low, high = (pieces[0], lax.ppermute(pieces[1], "xl", swap)), along_y(pieces[2:])
    keep, give, mine = halve(flat, low, high)
    beside, got, across = (
        lax.ppermute(array, XS, [(i, i ^ flip) for i in range(4)])
        for flip, array in ((1, mine), (2, give), (3, mine))
    )
    parts = mix(flat, keep, got, mine, beside, across, token_grad)
    out_grad, table_grad = final(exchange(parts, "z"))
    return (token_grad, out_grad.T, table_grad.T)


def solution(mesh):
    fine = Mesh(mesh.devices.reshape(2, 2, 8, 4, 2), ALL)
    grid = P(None, LAT, LON, None)
    return jax.shard_map(
        body,
        mesh=fine,
        in_specs=(grid, grid, P(), P(), P(), P()),
        out_specs=(grid, P(LAT, LON), P()),
        check_vma=False,
    )
```

```python
import functools

import jax
import jax.numpy as jnp
from jax import lax
from jax.experimental import pallas as pl
from jax.experimental.pallas import tpu as pltpu
from jax.sharding import Mesh
from jax.sharding import PartitionSpec as P

LEVELS = 2
WLAT = 6
WLON = 12
HALF_LAT = WLAT // 2
HALF_LON = WLON // 2
WIN = LEVELS * WLAT * WLON
PIECE = WIN // 4
HEADS = 16
HEAD = 64
D = HEADS * HEAD
NREL = 759
ROWS = 768
PARTS = ROWS // 128
SIDE = 6
TAIL = WIN - 128
STACK = WIN // SIDE
ROWS_PACKED = WIN + STACK
SCALE = HEAD ** (-0.5)
BF = jnp.bfloat16
F32 = jnp.float32
VMEM = pl.BlockSpec(memory_space=pltpu.VMEM)
ANY = pl.BlockSpec(memory_space=pl.ANY)
LAT = ("xh", "core")
LON = ("z", "y", "xl")
XS = ("xh", "xl")
ALL = ("xh", "core", "z", "y", "xl")

NT = (((1,), (1,)), ((), ()))
TN = (((0,), (0,)), ((), ()))


def dot(a, b, dims=(((1,), (0,)), ((), ()))):
    return lax.dot_general(a, b, dims, preferred_element_type=F32)


def place_x():
    return lax.axis_index("xh") * 2 + lax.axis_index("xl")


def params(mib):
    return pltpu.CompilerParams(vmem_limit_bytes=mib * 1024 * 1024)


def cost(flops, moved):
    return pl.CostEstimate(flops=flops, bytes_accessed=moved, transcendentals=0)


def groups():
    for level in range(LEVELS):
        for row in range(HALF_LAT):
            yield level, row, (level * HALF_LAT + row) * HALF_LON


def pack_kernel(tok, cot, lon_o, lat_o, dia_o, lon_s, lat_s, dia_s):
    for half, src in enumerate((tok, cot)):
        for level, row, at in groups():
            at = half * PIECE + at
            low = src[level, row].astype(F32)
            high = src[level, row + HALF_LAT].astype(F32)
            lon_s[at : at + HALF_LON] = high[:HALF_LON]
            dia_s[at : at + HALF_LON] = low[:HALF_LON]
            lat_s[at : at + HALF_LON] = low[HALF_LON:]
    lon_o[...] = lon_s[...].astype(BF)
    lat_o[...] = lat_s[...].astype(BF)
    dia_o[...] = dia_s[...].astype(BF)


def pack(tokens, cotangent):
    out = jax.ShapeDtypeStruct((2 * PIECE, D), BF)
    return pl.pallas_call(
        pack_kernel,
        out_shape=(out, out, out),
        in_specs=[VMEM, VMEM],
        out_specs=(VMEM, VMEM, VMEM),
        scratch_shapes=[pltpu.VMEM((2 * PIECE, D), F32)] * 3,
        compiler_params=params(4),
        cost_estimate=cost(1_000_000, 6_000_000),
        name="pack",
    )(tokens, cotangent)


def bias_kernel(table, rel, out, packed, table_s, rel_s, tail_s):
    table_s[:, :NREL] = table[...]
    rel_s[:, :TAIL] = rel[:, 128:]
    packed[:WIN] = rel[:, :128]
    lane = lax.broadcasted_iota(jnp.int32, (STACK, 128), 1)
    block = lane // TAIL
    tail = rel_s[:STACK]
    for side in range(1, SIDE):
        moved = pltpu.roll(rel_s[side * STACK : side * STACK + STACK], side * TAIL, 1)
        tail = jnp.where(block == side, moved, tail)
    packed[WIN:] = jnp.where(block < SIDE, tail, 0)
    free = lax.axis_index("xh") * 2 + lax.axis_index("core") < 3
    half = WIN // 2

    def wrapped(index):
        return lax.rem(index, half) >= half // 2

    row = lax.broadcasted_iota(jnp.int32, (8, 128), 0)
    col = lax.broadcasted_iota(jnp.int32, (8, 128), 1)

    def look_up(step):
        index = packed[pl.ds(pl.multiple_of(step * 8, 8), 8), :]
        low, high = index & 127, index >> 7
        masks = [high == part for part in range(PARTS)]
        for head in range(HEADS):
            total = jnp.zeros((8, 128), F32)
            for part in range(PARTS):
                line = table_s[head : head + 1, part * 128 : part * 128 + 128]
                source = jnp.broadcast_to(line, (8, 128))
                found = jnp.take_along_axis(source, low, axis=1, mode="promise_in_bounds")
                total = jnp.where(masks[part], found, total)
            yield head, total

    def main_rows(step, carry):
        allowed = jnp.logical_or(wrapped(row + step * 8) == wrapped(col), free)
        for head, total in look_up(step):
            out[head, pl.ds(pl.multiple_of(step * 8, 8), 8), :128] = jnp.where(
                allowed, total, -jnp.inf
            )
        return carry

    def tail_rows(step, carry):
        at = (step - WIN // 8) * 8
        allowed = jnp.logical_or(wrapped(col // TAIL * STACK + row + at), free)
        for head, total in look_up(step):
            tail_s[head, pl.ds(pl.multiple_of(at, 8), 8), :] = jnp.where(allowed, total, -jnp.inf)
        return carry

    lax.fori_loop(0, WIN // 8, main_rows, 0)
    lax.fori_loop(WIN // 8, ROWS_PACKED // 8, tail_rows, 0)
    for head in range(HEADS):
        found = tail_s[head]
        for side in range(SIDE):
            moved = found if side == 0 else pltpu.roll(found, 128 - side * TAIL, 1)
            out[head, side * STACK : side * STACK + STACK, 128:] = moved[:, :TAIL]


def bias_of(table, rel):
    return pl.pallas_call(
        bias_kernel,
        out_shape=(
            jax.ShapeDtypeStruct((HEADS, WIN, WIN), F32),
            jax.ShapeDtypeStruct((ROWS_PACKED, 128), jnp.int32),
        ),
        in_specs=[VMEM, VMEM],
        out_specs=(VMEM, VMEM),
        scratch_shapes=[
            pltpu.VMEM((HEADS, ROWS), F32),
            pltpu.VMEM((WIN, 128), jnp.int32),
            pltpu.VMEM((HEADS, STACK, 128), F32),
        ],
        compiler_params=params(4),
        cost_estimate=cost(10_000_000, 28_000_000),
        name="bias",
    )(table, rel)


def gather_window(out, own, lon, lat, dia, offset):
    for level, row, at in groups():
        at = at + offset
        base = level * WLAT * WLON + row * WLON
        out[base : base + HALF_LON] = own[level, row + HALF_LAT].astype(F32)[HALF_LON:]
        out[base + HALF_LON : base + WLON] = lon[at : at + HALF_LON]
        base = base + HALF_LAT * WLON
        out[base : base + HALF_LON] = lat[at : at + HALF_LON]
        out[base + HALF_LON : base + WLON] = dia[at : at + HALF_LON]


def forward_kernel(
    tok, cot, lon, lat, dia, bias, wqkv_hbm,
    cot_o, att_o, give_o, proj, probs_o, normed_o, std_o,
    att_s, x_s, c_s, lon_s, lat_s, dia_s, wqkv, sems,
):
    copies = [
        pltpu.make_async_copy(
            wqkv_hbm.at[:, pl.ds(part * D, D)], wqkv.at[part], sems.at[part]
        )
        for part in range(3)
    ]
    for copy in copies:
        copy.start()
    lon_s[...] = lon[...].astype(F32)
    lat_s[...] = lat[...].astype(F32)
    dia_s[...] = dia[...].astype(F32)
    gather_window(x_s, tok, lon_s, lat_s, dia_s, 0)
    gather_window(c_s, cot, lon_s, lat_s, dia_s, PIECE)
    cot_o[...] = c_s[...].astype(BF)
    x = x_s[...]
    centred = x - jnp.mean(x, axis=1, keepdims=True)
    inv_std = lax.rsqrt(jnp.mean(centred * centred, axis=1, keepdims=True) + 1e-05)
    normed = centred * inv_std
    normed_o[...] = normed
    std_o[...] = jnp.broadcast_to(inv_std, (WIN, 128))
    hidden = normed.astype(BF)
    for part in range(3):
        copies[part].wait()
        proj[part] = dot(hidden, wqkv[part]).astype(BF)
    lane = lax.broadcasted_iota(jnp.int32, (WIN, 128), 1)
    masks = (lane < HEAD, lane >= HEAD)
    zero = jnp.zeros((WIN, 128), BF)

    for pair in range(HEADS // 2):
        lanes = slice(pair * 128, pair * 128 + 128)
        query = proj[0, :, lanes]
        key = proj[1, :, lanes]
        value = proj[2, :, lanes]
        attended = []
        for side in (0, 1):
            head = pair * 2 + side
            scores = dot(jnp.where(masks[side], query, zero), key, NT) * SCALE + bias[head]
            expo = jnp.exp(scores - jnp.max(scores, axis=1, keepdims=True))
            probs = expo * (1.0 / jnp.sum(expo, axis=1, keepdims=True))
            probs_o[head, :WIN] = probs[:, :128]
            probs_o[head, WIN:, : WIN - 128] = probs[:, 128:]
            attended.append(dot(probs.astype(BF), value))
        block, core = pair // 4, (pair // 2) % 2
        at = block * 256 + (pair % 2) * 128
        att_s[core, :, at : at + 128] = jnp.where(masks[0], attended[0], attended[1]).astype(BF)
    place = lax.axis_index("core")
    att_o[...] = att_s[place]
    give_o[:, : D // 2] = att_s[1 - place]
    give_o[:, D // 2 :] = cot_o[...]


def forward(tokens, cotangent, lon, lat, dia, bias, qkv_weight):
    return pl.pallas_call(
        forward_kernel,
        out_shape=(
            jax.ShapeDtypeStruct((WIN, D), BF),
            jax.ShapeDtypeStruct((WIN, D // 2), BF),
            jax.ShapeDtypeStruct((WIN, D // 2 + D), BF),
            jax.ShapeDtypeStruct((3, WIN, D), BF),
            jax.ShapeDtypeStruct((HEADS, 2 * WIN, 128), F32),
            jax.ShapeDtypeStruct((WIN, D), F32),
            jax.ShapeDtypeStruct((WIN, 128), F32),
        ),
        in_specs=[VMEM] * 6 + [ANY],
        out_specs=(VMEM,) * 7,
        scratch_shapes=[
            pltpu.VMEM((2, WIN, D // 2), BF),
            pltpu.VMEM((WIN, D), F32),
            pltpu.VMEM((WIN, D), F32),
            pltpu.VMEM((2 * PIECE, D), F32),
            pltpu.VMEM((2 * PIECE, D), F32),
            pltpu.VMEM((2 * PIECE, D), F32),
            pltpu.VMEM((3, D, D), BF),
            pltpu.SemaphoreType.DMA((3,)),
        ],
        compiler_params=params(44),
        cost_estimate=cost(1_000_000_000, 15_000_000),
        name="forward",
    )(tokens, cotangent, lon, lat, dia, bias, qkv_weight)


def scores_kernel(
    cot, wout, probs, proj, after, gatt, ph_o, ds_o, grads
):
    gatt[...] = dot(cot[...], wout[...], NT).astype(BF)
    blank = jnp.zeros((WIN, 128 - TAIL), F32)
    lane = lax.broadcasted_iota(jnp.int32, (WIN, 128), 1)
    masks = (lane < HEAD, lane >= HEAD)
    zero = jnp.zeros((WIN, 128), BF)
    for pair in range(HEADS // 2):
        lanes = slice(pair * 128, pair * 128 + 128)
        value = proj[2, :, lanes]
        grad = gatt[:, lanes]
        for side in (0, 1):
            head = pair * 2 + side
            prob = jnp.concatenate(
                [probs[head, :WIN], probs[head, WIN:, : WIN - 128]], axis=1
            )
            ph_o[head] = prob.astype(BF)
            grad_probs = dot(jnp.where(masks[side], grad, zero), value, NT)
            inner = jnp.sum(prob * grad_probs, axis=1, keepdims=True)
            grad_scores = prob * (grad_probs - inner)
            ds_o[head] = (grad_scores * SCALE).astype(BF)
            grads[head, :WIN] = grad_scores[:, :128]
            tail = jnp.concatenate([grad_scores[:, 128:], blank], axis=1)
            packed = tail[:STACK]
            for at in range(1, SIDE):
                packed = packed + pltpu.roll(tail[at * STACK : at * STACK + STACK], at * TAIL, 1)
            grads[head, WIN:] = packed


def score_grads(cot, out_weight, probs, proj, after):
    square = jax.ShapeDtypeStruct((HEADS, WIN, WIN), BF)
    return pl.pallas_call(
        scores_kernel,
        out_shape=(
            jax.ShapeDtypeStruct((WIN, D), BF),
            square,
            square,
            jax.ShapeDtypeStruct((HEADS, ROWS_PACKED, 128), F32),
        ),
        in_specs=[VMEM] * 4 + [ANY],
        out_specs=(VMEM,) * 4,
        compiler_params=params(8),
        cost_estimate=cost(1_000_000_000, 16_000_000),
        name="score_grads",
    )(cot, out_weight, probs, proj, after)


def backward_kernel(
    cot, std, wqkv, proj, gatt, ph, ds, normed, after, own_o, lon_o, lat_o,
    stacked, grad_s, piece_s,
):
    first = lax.broadcasted_iota(jnp.int32, (WIN, 128), 1) < HEAD
    for pair in range(HEADS // 2):
        lanes = slice(pair * 128, pair * 128 + 128)
        query = proj[0, :, lanes]
        key = proj[1, :, lanes]
        grad = gatt[:, lanes]
        found = ([], [], [])
        for side in (0, 1):
            head = pair * 2 + side
            weights = ds[head]
            found[0].append(dot(weights, key))
            found[1].append(dot(weights, query, TN))
            found[2].append(dot(ph[head], grad, TN))
        for part in range(3):
            stacked[part, :, lanes] = jnp.where(first, *found[part]).astype(BF)
    total = jnp.zeros((WIN, D), F32)
    for part in range(3):
        total = total + dot(stacked[part], wqkv[:, part * D : part * D + D], NT)
    norm = normed[...]
    branch = (
        total
        - jnp.mean(total, axis=1, keepdims=True)
        - norm * jnp.mean(total * norm, axis=1, keepdims=True)
    ) * std[:, :1]
    grad_s[...] = cot[...].astype(F32) + branch
    for which in (0, 2, 1, 3):
        shift = (which // 2) * HALF_LAT * WLON + (which % 2) * HALF_LON
        for level, row, at in groups():
            base = level * WLAT * WLON + row * WLON + shift
            at = at + (PIECE if which == 3 else 0)
            piece_s[at : at + HALF_LON] = grad_s[base : base + HALF_LON]
        if which % 2 == 0:
            (own_o, lat_o)[which // 2][...] = piece_s[:PIECE].astype(BF)
    lon_o[...] = piece_s[...].astype(BF)


def backward(cot, std, qkv_weight, proj, gatt, ph, ds, normed, after):
    piece = jax.ShapeDtypeStruct((PIECE, D), BF)
    return pl.pallas_call(
        backward_kernel,
        out_shape=(piece, jax.ShapeDtypeStruct((2 * PIECE, D), BF), piece),
        in_specs=[VMEM] * 8 + [ANY],
        out_specs=(VMEM,) * 3,
        scratch_shapes=[
            pltpu.VMEM((3, WIN, D), BF),
            pltpu.VMEM((WIN, D), F32),
            pltpu.VMEM((2 * PIECE, D), F32),
        ],
        compiler_params=params(8),
        cost_estimate=cost(1_000_000_000, 16_000_000),
        name="backward",
    )(cot, std, qkv_weight, proj, gatt, ph, ds, normed, after)


def table_kernel(grads, packed, out):
    lane_id = lax.broadcasted_iota(jnp.int32, (128, 128), 0)

    def two_rows(step, total):
        hots, grad_rows, blocks = [], [], []
        for which in (0, 1):
            row = step * 2 + which
            index = packed[pl.ds(row, 1), :]
            hots.append(jnp.where(lane_id == (index & 127), 1.0, 0.0).astype(BF))
            grad_rows.append(grads[pl.ds(row, HEADS, stride=ROWS_PACKED), :])
            blocks.append(index >> 7)
        grad = jnp.concatenate(grad_rows, axis=1)
        block = jnp.concatenate(blocks, axis=1)
        picked = jnp.concatenate(
            [jnp.where(block == part, grad, 0.0) for part in range(PARTS)], axis=0
        )
        return total + dot(picked.astype(BF), jnp.concatenate(hots, axis=1), NT)

    total = lax.fori_loop(
        0, ROWS_PACKED // 2, two_rows, jnp.zeros((PARTS * HEADS, 128), F32), unroll=4
    )
    total = total.astype(BF)
    for part in range(PARTS):
        at = part % 2 * 128
        out[part // 2, :, at : at + 128] = total[part * HEADS : part * HEADS + HEADS]


def table_of(grads, packed):
    return pl.pallas_call(
        table_kernel,
        out_shape=jax.ShapeDtypeStruct((PARTS // 2, HEADS, 256), BF),
        in_specs=[VMEM, VMEM],
        out_specs=VMEM,
        compiler_params=params(4),
        cost_estimate=cost(1_000, 1_000),
        name="table",
    )(grads.reshape(HEADS * ROWS_PACKED, 128), packed)


def added(pieces):
    total = pieces[0][...].astype(F32)
    for piece in pieces[1:]:
        total = total + piece[...].astype(F32)
    return total


def slots(ref):
    return [ref.at[i] for i in range(ref.shape[0])]


def outer_kernel(cot, att, far, *refs):
    outs, total_s = refs[:-1], refs[-1]
    cuts, depth = total_s.shape[:2]
    total = dot(cot[...], att[...], TN) + dot(far[:, D // 2 :], far[:, : D // 2], TN)
    total = total.astype(BF).reshape(depth, cuts, 32, D // 2)
    for y in range(cuts):
        total_s[y] = total[:, y]
    for step, out in enumerate(outs):
        out[...] = total_s[lax.rem(lax.axis_index("y") + step, cuts)]


def outer(cuts, depth, cot, att, far):
    shape = (depth, 32, D // 2)
    return pl.pallas_call(
        outer_kernel,
        out_shape=(jax.ShapeDtypeStruct(shape, BF),) * cuts,
        in_specs=[VMEM] * 3,
        out_specs=(VMEM,) * cuts,
        scratch_shapes=[pltpu.VMEM((cuts,) + shape, BF)],
        compiler_params=params(8),
        cost_estimate=cost(600_000_000, 3_000_000),
        name="outer",
    )(cot, att, far)


def first_kernel(*refs):
    pieces, tables, (total, table) = refs[:4], refs[4:6], refs[7:]
    total[...] = added(pieces).astype(BF)
    table[...] = added(tables).astype(BF)


def first_sums(pieces, tables, after):
    return pl.pallas_call(
        first_kernel,
        out_shape=(
            jax.ShapeDtypeStruct(pieces[0].shape, BF),
            jax.ShapeDtypeStruct(tables[0].shape, BF),
        ),
        in_specs=[VMEM] * 6 + [ANY],
        out_specs=(VMEM,) * 2,
        compiler_params=params(4),
        name="first_sums",
    )(*pieces, *tables, after)


def turn_kernel(total, *refs):
    tables, outs, (total_s, table_s) = refs[:4], refs[4:8], refs[8:]
    depth = total_s.shape[1]
    for xh in range(2):
        for xl in range(2):
            total_s[xh * 2 + xl] = total[:, xl * 16 : xl * 16 + 16, xh * 256 : xh * 256 + 256]
    for step, ref in enumerate(tables):
        table_s[lax.rem(lax.axis_index("y") + 4 - step, 4)] = ref[...]
    table = added(slots(table_s)).astype(BF)
    for flip, out in enumerate(outs):
        out[:depth] = total_s[place_x() ^ flip]
        out[depth:] = table


def turn(total, tables):
    depth, table = total.shape[0], tables[0].shape
    out = jax.ShapeDtypeStruct((depth + table[0], 16, 256), BF)
    return pl.pallas_call(
        turn_kernel,
        out_shape=(out,) * 4,
        in_specs=[VMEM] * 5,
        out_specs=(VMEM,) * 4,
        scratch_shapes=[pltpu.VMEM((4, depth, 16, 256), BF), pltpu.VMEM((4,) + table, BF)],
        compiler_params=params(4),
        name="turn",
    )(total, *tables)


def mix_kernel(*refs):
    pieces, (after, out, table_s) = refs[:4], refs[4:]
    depth = out.shape[0]
    for flip, ref in enumerate(pieces):
        table_s[place_x() ^ flip] = ref[depth:]
    table = added(slots(table_s)).astype(BF)
    out[:, 0] = added([ref.at[:depth] for ref in pieces]).astype(BF)
    for z in range(depth):
        out[z, 1:] = table


def mix(pieces, after):
    rows = PARTS // 2
    return pl.pallas_call(
        mix_kernel,
        out_shape=jax.ShapeDtypeStruct((pieces[0].shape[0] - rows, 1 + rows, 16, 256), BF),
        in_specs=[VMEM] * 4 + [ANY],
        out_specs=VMEM,
        scratch_shapes=[pltpu.VMEM((4, rows, 16, 256), BF)],
        compiler_params=params(4),
        name="mix",
    )(*pieces, after)


def final_kernel(pieces, out, table):
    total = added(slots(pieces))
    out[...] = total[0]
    for part in range(PARTS):
        at = part % 2 * 128
        lanes = min(128, NREL - part * 128)
        table[:, part * 128 : part * 128 + lanes] = total[1 + part // 2, :, at : at + lanes]


def final(pieces):
    return pl.pallas_call(
        final_kernel,
        out_shape=(
            jax.ShapeDtypeStruct((16, 256), F32),
            jax.ShapeDtypeStruct((HEADS, NREL), F32),
        ),
        in_specs=[VMEM],
        out_specs=(VMEM,) * 2,
        compiler_params=params(4),
        name="final",
    )(pieces)


def join_kernel(own, lon, lat, out, own_s, lon_s, lat_s, line):
    own_s[...] = own[...].astype(F32)
    lon_s[...] = lon[...].astype(F32)
    lat_s[...] = lat[...].astype(F32)
    for level, row, at in groups():
        line[:HALF_LON] = lat_s[at + PIECE : at + PIECE + HALF_LON]
        line[HALF_LON:] = lat_s[at : at + HALF_LON]
        out[level, row] = line[...].astype(BF)
        line[:HALF_LON] = lon_s[at : at + HALF_LON]
        line[HALF_LON:] = own_s[at : at + HALF_LON]
        out[level, row + HALF_LAT] = line[...].astype(BF)


def join(own, lon, lat):
    return pl.pallas_call(
        join_kernel,
        out_shape=jax.ShapeDtypeStruct((LEVELS, WLAT, WLON, D), BF),
        in_specs=[VMEM] * 3,
        out_specs=VMEM,
        scratch_shapes=[
            pltpu.VMEM((PIECE, D), F32),
            pltpu.VMEM((2 * PIECE, D), F32),
            pltpu.VMEM((2 * PIECE, D), F32),
            pltpu.VMEM((WLON, D), F32),
        ],
        compiler_params=params(4),
        name="join",
    )(own, lon, lat)


def shift(array, axes, by):
    peers = lax.axis_size(axes)
    return lax.ppermute(array, axes, [(i, (i + by) % peers) for i in range(peers)])


def shift_both(array, by):
    lats, lons = lax.axis_size(LAT), lax.axis_size(LON)
    pairs = [
        (a * lons + b, ((a + by) % lats) * lons + (b + by) % lons)
        for a in range(lats)
        for b in range(lons)
    ]
    return lax.ppermute(array, ALL, pairs)


def exchange(pieces, axes):
    return lax.all_to_all(pieces, axes, 0, 0, tiled=True)


def along_y(pieces):
    return [pieces[0]] + [shift(pieces[step], "y", step) for step in range(1, 4)]


def along_x(pieces):
    flips = [[(i, i ^ flip) for i in range(4)] for flip in range(4)]
    return [pieces[0]] + [lax.ppermute(pieces[flip], XS, flips[flip]) for flip in range(1, 4)]


def body(tokens, cotangent, qkv_weight, out_weight, bias_table, rel_index):
    swap = [(0, 1), (1, 0)]
    send = pack(tokens, cotangent)
    lon = shift(send[0], LON, -1)
    lat = shift(send[1], LAT, -1)
    dia = shift_both(send[2], -1)
    bias, packed = bias_of(bias_table.T, rel_index)
    cot, att, give, proj, probs, normed, std = forward(
        tokens, cotangent, lon, lat, dia, bias, qkv_weight
    )
    far = lax.ppermute(give, "core", swap)
    pieces = outer(lax.axis_size("y"), lax.axis_size("z"), cot, att, far)
    gatt, ph, ds, grads = score_grads(cot, out_weight, probs, proj, pieces[0])
    table = table_of(grads, packed)
    own, lon, lat = backward(cot, std, qkv_weight, proj, gatt, ph, ds, normed, table)
    far = lax.ppermute(table, "core", swap)
    total, table = first_sums(along_y(pieces), (table, far), own)
    pieces = along_x(turn(total, along_y([table] * 4)))
    lon = shift(lon, LON, 1)
    parts = mix(pieces, lon)
    lat = shift(jnp.concatenate([lat, lon[PIECE:]], axis=0), LAT, 1)
    out_grad, table_grad = final(exchange(parts, "z"))
    return (join(own, lon, lat), out_grad.T, table_grad.T)


def solution(mesh):
    fine = Mesh(mesh.devices.reshape(2, 2, 8, 4, 2), ALL)
    grid = P(None, LAT, LON, None)
    return jax.shard_map(
        body,
        mesh=fine,
        in_specs=(grid, grid, P(), P(), P(), P()),
        out_specs=(grid, P(LAT, LON), P()),
        check_vma=False,
    )
```

```python
import functools

import jax
import jax.numpy as jnp
from jax import lax
from jax.experimental import pallas as pl
from jax.experimental.pallas import tpu as pltpu
from jax.sharding import Mesh
from jax.sharding import PartitionSpec as P

LEVELS = 2
WLAT = 6
WLON = 12
HALF_LAT = WLAT // 2
HALF_LON = WLON // 2
WIN = LEVELS * WLAT * WLON
PIECE = WIN // 4
HEADS = 16
HEAD = 64
D = HEADS * HEAD
NREL = 759
ROWS = 768
PARTS = ROWS // 128
SIDE = 6
TAIL = WIN - 128
STACK = WIN // SIDE
ROWS_PACKED = WIN + STACK
SCALE = HEAD ** (-0.5)
BF = jnp.bfloat16
F32 = jnp.float32
VMEM = pl.BlockSpec(memory_space=pltpu.VMEM)
ANY = pl.BlockSpec(memory_space=pl.ANY)
LAT = ("xh", "core")
LON = ("z", "y", "xl")
XS = ("xh", "xl")
ALL = ("xh", "core", "z", "y", "xl")

NT = (((1,), (1,)), ((), ()))
TN = (((0,), (0,)), ((), ()))


def dot(a, b, dims=(((1,), (0,)), ((), ()))):
    return lax.dot_general(a, b, dims, preferred_element_type=F32)


def place_x():
    return lax.axis_index("xh") * 2 + lax.axis_index("xl")


def params(mib):
    return pltpu.CompilerParams(vmem_limit_bytes=mib * 1024 * 1024)


def cost(flops, moved):
    return pl.CostEstimate(flops=flops, bytes_accessed=moved, transcendentals=0)


def groups():
    for level in range(LEVELS):
        for row in range(HALF_LAT):
            yield level, row, (level * HALF_LAT + row) * HALF_LON


def pack_kernel(tok, cot, lon_o, lat_o, dia_o, lon_s, lat_s, dia_s):
    for half, src in enumerate((tok, cot)):
        for level, row, at in groups():
            at = half * PIECE + at
            low = src[level, row].astype(F32)
            high = src[level, row + HALF_LAT].astype(F32)
            lon_s[at : at + HALF_LON] = high[:HALF_LON]
            dia_s[at : at + HALF_LON] = low[:HALF_LON]
            lat_s[at : at + HALF_LON] = low[HALF_LON:]
    lon_o[...] = lon_s[...].astype(BF)
    lat_o[...] = lat_s[...].astype(BF)
    dia_o[...] = dia_s[...].astype(BF)


def pack(tokens, cotangent):
    out = jax.ShapeDtypeStruct((2 * PIECE, D), BF)
    return pl.pallas_call(
        pack_kernel,
        out_shape=(out, out, out),
        in_specs=[VMEM, VMEM],
        out_specs=(VMEM, VMEM, VMEM),
        scratch_shapes=[pltpu.VMEM((2 * PIECE, D), F32)] * 3,
        compiler_params=params(4),
        cost_estimate=cost(1_000_000, 6_000_000),
        name="pack",
    )(tokens, cotangent)


def bias_kernel(table, rel, out, packed, table_s, rel_s, tail_s):
    table_s[:, :NREL] = table[...]
    rel_s[:, :TAIL] = rel[:, 128:]
    packed[:WIN] = rel[:, :128]
    lane = lax.broadcasted_iota(jnp.int32, (STACK, 128), 1)
    block = lane // TAIL
    tail = rel_s[:STACK]
    for side in range(1, SIDE):
        moved = pltpu.roll(rel_s[side * STACK : side * STACK + STACK], side * TAIL, 1)
        tail = jnp.where(block == side, moved, tail)
    packed[WIN:] = jnp.where(block < SIDE, tail, 0)
    free = lax.axis_index("xh") * 2 + lax.axis_index("core") < 3
    half = WIN // 2

    def wrapped(index):
        return lax.rem(index, half) >= half // 2

    row = lax.broadcasted_iota(jnp.int32, (8, 128), 0)
    col = lax.broadcasted_iota(jnp.int32, (8, 128), 1)

    def look_up(step):
        index = packed[pl.ds(pl.multiple_of(step * 8, 8), 8), :]
        low, high = index & 127, index >> 7
        masks = [high == part for part in range(PARTS)]
        for head in range(HEADS):
            total = jnp.zeros((8, 128), F32)
            for part in range(PARTS):
                line = table_s[head : head + 1, part * 128 : part * 128 + 128]
                source = jnp.broadcast_to(line, (8, 128))
                found = jnp.take_along_axis(source, low, axis=1, mode="promise_in_bounds")
                total = jnp.where(masks[part], found, total)
            yield head, total

    def main_rows(step, carry):
        allowed = jnp.logical_or(wrapped(row + step * 8) == wrapped(col), free)
        for head, total in look_up(step):
            out[head, pl.ds(pl.multiple_of(step * 8, 8), 8), :128] = jnp.where(
                allowed, total, -jnp.inf
            )
        return carry

    def tail_rows(step, carry):
        at = (step - WIN // 8) * 8
        allowed = jnp.logical_or(wrapped(col // TAIL * STACK + row + at), free)
        for head, total in look_up(step):
            tail_s[head, pl.ds(pl.multiple_of(at, 8), 8), :] = jnp.where(allowed, total, -jnp.inf)
        return carry

    lax.fori_loop(0, WIN // 8, main_rows, 0)
    lax.fori_loop(WIN // 8, ROWS_PACKED // 8, tail_rows, 0)
    for head in range(HEADS):
        found = tail_s[head]
        for side in range(SIDE):
            moved = found if side == 0 else pltpu.roll(found, 128 - side * TAIL, 1)
            out[head, side * STACK : side * STACK + STACK, 128:] = moved[:, :TAIL]


def bias_of(table, rel):
    return pl.pallas_call(
        bias_kernel,
        out_shape=(
            jax.ShapeDtypeStruct((HEADS, WIN, WIN), F32),
            jax.ShapeDtypeStruct((ROWS_PACKED, 128), jnp.int32),
        ),
        in_specs=[VMEM, VMEM],
        out_specs=(VMEM, VMEM),
        scratch_shapes=[
            pltpu.VMEM((HEADS, ROWS), F32),
            pltpu.VMEM((WIN, 128), jnp.int32),
            pltpu.VMEM((HEADS, STACK, 128), F32),
        ],
        compiler_params=params(4),
        cost_estimate=cost(10_000_000, 28_000_000),
        name="bias",
    )(table, rel)


def gather_window(out, own, lon, lat, dia, offset):
    for level, row, at in groups():
        at = at + offset
        base = level * WLAT * WLON + row * WLON
        out[base : base + HALF_LON] = own[level, row + HALF_LAT].astype(F32)[HALF_LON:]
        out[base + HALF_LON : base + WLON] = lon[at : at + HALF_LON]
        base = base + HALF_LAT * WLON
        out[base : base + HALF_LON] = lat[at : at + HALF_LON]
        out[base + HALF_LON : base + WLON] = dia[at : at + HALF_LON]


def forward_kernel(
    tok, cot, lon, lat, dia, bias, wqkv_hbm,
    cot_o, att_o, give_o, proj, probs_o, normed_o, std_o,
    att_s, x_s, c_s, lon_s, lat_s, dia_s, wqkv, sems,
):
    copies = [
        pltpu.make_async_copy(
            wqkv_hbm.at[:, pl.ds(part * D, D)], wqkv.at[part], sems.at[part]
        )
        for part in range(3)
    ]
    for copy in copies:
        copy.start()
    lon_s[...] = lon[...].astype(F32)
    lat_s[...] = lat[...].astype(F32)
    dia_s[...] = dia[...].astype(F32)
    gather_window(x_s, tok, lon_s, lat_s, dia_s, 0)
    gather_window(c_s, cot, lon_s, lat_s, dia_s, PIECE)
    cot_o[...] = c_s[...].astype(BF)
    x = x_s[...]
    centred = x - jnp.mean(x, axis=1, keepdims=True)
    inv_std = lax.rsqrt(jnp.mean(centred * centred, axis=1, keepdims=True) + 1e-05)
    normed = centred * inv_std
    normed_o[...] = normed
    std_o[...] = jnp.broadcast_to(inv_std, (WIN, 128))
    hidden = normed.astype(BF)
    for part in range(3):
        copies[part].wait()
        proj[part] = dot(hidden, wqkv[part]).astype(BF)
    lane = lax.broadcasted_iota(jnp.int32, (WIN, 128), 1)
    masks = (lane < HEAD, lane >= HEAD)
    zero = jnp.zeros((WIN, 128), BF)

    for pair in range(HEADS // 2):
        lanes = slice(pair * 128, pair * 128 + 128)
        query = proj[0, :, lanes]
        key = proj[1, :, lanes]
        value = proj[2, :, lanes]
        attended = []
        for side in (0, 1):
            head = pair * 2 + side
            scores = dot(jnp.where(masks[side], query, zero), key, NT) * SCALE + bias[head]
            expo = jnp.exp(scores - jnp.max(scores, axis=1, keepdims=True))
            probs = expo * (1.0 / jnp.sum(expo, axis=1, keepdims=True))
            probs_o[head, :WIN] = probs[:, :128]
            probs_o[head, WIN:, : WIN - 128] = probs[:, 128:]
            attended.append(dot(probs.astype(BF), value))
        block, core = pair // 4, (pair // 2) % 2
        at = block * 256 + (pair % 2) * 128
        att_s[core, :, at : at + 128] = jnp.where(masks[0], attended[0], attended[1]).astype(BF)
    place = lax.axis_index("core")
    att_o[...] = att_s[place]
    give_o[:, : D // 2] = att_s[1 - place]
    give_o[:, D // 2 :] = cot_o[...]


def forward(tokens, cotangent, lon, lat, dia, bias, qkv_weight):
    return pl.pallas_call(
        forward_kernel,
        out_shape=(
            jax.ShapeDtypeStruct((WIN, D), BF),
            jax.ShapeDtypeStruct((WIN, D // 2), BF),
            jax.ShapeDtypeStruct((WIN, D // 2 + D), BF),
            jax.ShapeDtypeStruct((3, WIN, D), BF),
            jax.ShapeDtypeStruct((HEADS, 2 * WIN, 128), F32),
            jax.ShapeDtypeStruct((WIN, D), F32),
            jax.ShapeDtypeStruct((WIN, 128), F32),
        ),
        in_specs=[VMEM] * 6 + [ANY],
        out_specs=(VMEM,) * 7,
        scratch_shapes=[
            pltpu.VMEM((2, WIN, D // 2), BF),
            pltpu.VMEM((WIN, D), F32),
            pltpu.VMEM((WIN, D), F32),
            pltpu.VMEM((2 * PIECE, D), F32),
            pltpu.VMEM((2 * PIECE, D), F32),
            pltpu.VMEM((2 * PIECE, D), F32),
            pltpu.VMEM((3, D, D), BF),
            pltpu.SemaphoreType.DMA((3,)),
        ],
        compiler_params=params(44),
        cost_estimate=cost(1_000_000_000, 15_000_000),
        name="forward",
    )(tokens, cotangent, lon, lat, dia, bias, qkv_weight)


def grad_att_kernel(cot, wout, out):
    out[...] = dot(cot[...], wout[...], NT).astype(BF)


def grad_att(cot, out_weight):
    return pl.pallas_call(
        grad_att_kernel,
        out_shape=jax.ShapeDtypeStruct((WIN, D), BF),
        in_specs=[VMEM] * 2,
        out_specs=VMEM,
        compiler_params=params(8),
        cost_estimate=cost(300_000_000, 4_000_000),
        name="grad_att",
    )(cot, out_weight)


def scores_kernel(gatt, probs, proj, after, ph_o, ds_o, grads):
    blank = jnp.zeros((WIN, 128 - TAIL), F32)
    lane = lax.broadcasted_iota(jnp.int32, (WIN, 128), 1)
    masks = (lane < HEAD, lane >= HEAD)
    zero = jnp.zeros((WIN, 128), BF)
    for pair in range(HEADS // 2):
        lanes = slice(pair * 128, pair * 128 + 128)
        value = proj[2, :, lanes]
        grad = gatt[:, lanes]
        for side in (0, 1):
            head = pair * 2 + side
            prob = jnp.concatenate(
                [probs[head, :WIN], probs[head, WIN:, : WIN - 128]], axis=1
            )
            ph_o[head] = prob.astype(BF)
            grad_probs = dot(jnp.where(masks[side], grad, zero), value, NT)
            inner = jnp.sum(prob * grad_probs, axis=1, keepdims=True)
            grad_scores = prob * (grad_probs - inner)
            ds_o[head] = (grad_scores * SCALE).astype(BF)
            grads[head, :WIN] = grad_scores[:, :128]
            tail = jnp.concatenate([grad_scores[:, 128:], blank], axis=1)
            packed = tail[:STACK]
            for at in range(1, SIDE):
                packed = packed + pltpu.roll(tail[at * STACK : at * STACK + STACK], at * TAIL, 1)
            grads[head, WIN:] = packed


def score_grads(gatt, probs, proj, after):
    square = jax.ShapeDtypeStruct((HEADS, WIN, WIN), BF)
    return pl.pallas_call(
        scores_kernel,
        out_shape=(
            square,
            square,
            jax.ShapeDtypeStruct((HEADS, ROWS_PACKED, 128), F32),
        ),
        in_specs=[VMEM] * 3 + [ANY],
        out_specs=(VMEM,) * 3,
        compiler_params=params(8),
        cost_estimate=cost(1_000_000_000, 16_000_000),
        name="score_grads",
    )(gatt, probs, proj, after)


def backward_kernel(
    cot, std, wqkv, proj, gatt, ph, ds, normed, after, own_o, lon_o, lat_o,
    stacked, grad_s, piece_s,
):
    first = lax.broadcasted_iota(jnp.int32, (WIN, 128), 1) < HEAD
    for pair in range(HEADS // 2):
        lanes = slice(pair * 128, pair * 128 + 128)
        query = proj[0, :, lanes]
        key = proj[1, :, lanes]
        grad = gatt[:, lanes]
        found = ([], [], [])
        for side in (0, 1):
            head = pair * 2 + side
            weights = ds[head]
            found[0].append(dot(weights, key))
            found[1].append(dot(weights, query, TN))
            found[2].append(dot(ph[head], grad, TN))
        for part in range(3):
            stacked[part, :, lanes] = jnp.where(first, *found[part]).astype(BF)
    total = jnp.zeros((WIN, D), F32)
    for part in range(3):
        total = total + dot(stacked[part], wqkv[:, part * D : part * D + D], NT)
    norm = normed[...]
    branch = (
        total
        - jnp.mean(total, axis=1, keepdims=True)
        - norm * jnp.mean(total * norm, axis=1, keepdims=True)
    ) * std[:, :1]
    grad_s[...] = cot[...].astype(F32) + branch
    for which in (0, 2, 1, 3):
        shift = (which // 2) * HALF_LAT * WLON + (which % 2) * HALF_LON
        for level, row, at in groups():
            base = level * WLAT * WLON + row * WLON + shift
            at = at + (PIECE if which == 3 else 0)
            piece_s[at : at + HALF_LON] = grad_s[base : base + HALF_LON]
        if which % 2 == 0:
            (own_o, lat_o)[which // 2][...] = piece_s[:PIECE].astype(BF)
    lon_o[...] = piece_s[...].astype(BF)


def backward(cot, std, qkv_weight, proj, gatt, ph, ds, normed, after):
    piece = jax.ShapeDtypeStruct((PIECE, D), BF)
    return pl.pallas_call(
        backward_kernel,
        out_shape=(piece, jax.ShapeDtypeStruct((2 * PIECE, D), BF), piece),
        in_specs=[VMEM] * 8 + [ANY],
        out_specs=(VMEM,) * 3,
        scratch_shapes=[
            pltpu.VMEM((3, WIN, D), BF),
            pltpu.VMEM((WIN, D), F32),
            pltpu.VMEM((2 * PIECE, D), F32),
        ],
        compiler_params=params(8),
        cost_estimate=cost(1_000_000_000, 16_000_000),
        name="backward",
    )(cot, std, qkv_weight, proj, gatt, ph, ds, normed, after)


def table_kernel(grads, packed, out):
    lane_id = lax.broadcasted_iota(jnp.int32, (128, 128), 0)

    def two_rows(step, total):
        hots, grad_rows, blocks = [], [], []
        for which in (0, 1):
            row = step * 2 + which
            index = packed[pl.ds(row, 1), :]
            hots.append(jnp.where(lane_id == (index & 127), 1.0, 0.0).astype(BF))
            grad_rows.append(grads[pl.ds(row, HEADS, stride=ROWS_PACKED), :])
            blocks.append(index >> 7)
        grad = jnp.concatenate(grad_rows, axis=1)
        block = jnp.concatenate(blocks, axis=1)
        picked = jnp.concatenate(
            [jnp.where(block == part, grad, 0.0) for part in range(PARTS)], axis=0
        )
        return total + dot(picked.astype(BF), jnp.concatenate(hots, axis=1), NT)

    total = lax.fori_loop(
        0, ROWS_PACKED // 2, two_rows, jnp.zeros((PARTS * HEADS, 128), F32), unroll=4
    )
    total = total.astype(BF)
    for part in range(PARTS):
        at = part % 2 * 128
        out[part // 2, :, at : at + 128] = total[part * HEADS : part * HEADS + HEADS]


def table_of(grads, packed):
    return pl.pallas_call(
        table_kernel,
        out_shape=jax.ShapeDtypeStruct((PARTS // 2, HEADS, 256), BF),
        in_specs=[VMEM, VMEM],
        out_specs=VMEM,
        compiler_params=params(4),
        cost_estimate=cost(1_000, 1_000),
        name="table",
    )(grads.reshape(HEADS * ROWS_PACKED, 128), packed)


def added(pieces):
    total = pieces[0][...].astype(F32)
    for piece in pieces[1:]:
        total = total + piece[...].astype(F32)
    return total


def slots(ref):
    return [ref.at[i] for i in range(ref.shape[0])]


def outer_kernel(cot, att, far, after, *refs):
    outs, total_s = refs[:-1], refs[-1]
    cuts, depth = total_s.shape[:2]
    total = dot(cot[...], att[...], TN) + dot(far[:, D // 2 :], far[:, : D // 2], TN)
    total = total.astype(BF).reshape(depth, cuts, 32, D // 2)
    for y in range(cuts):
        total_s[y] = total[:, y]
    for step, out in enumerate(outs):
        out[...] = total_s[lax.rem(lax.axis_index("y") + step, cuts)]


def outer(cuts, depth, cot, att, far, after):
    shape = (depth, 32, D // 2)
    return pl.pallas_call(
        outer_kernel,
        out_shape=(jax.ShapeDtypeStruct(shape, BF),) * cuts,
        in_specs=[VMEM] * 3 + [ANY],
        out_specs=(VMEM,) * cuts,
        scratch_shapes=[pltpu.VMEM((cuts,) + shape, BF)],
        compiler_params=params(8),
        cost_estimate=cost(600_000_000, 3_000_000),
        name="outer",
    )(cot, att, far, after)


def first_kernel(*refs):
    pieces, tables, (total, table) = refs[:4], refs[4:6], refs[7:]
    total[...] = added(pieces).astype(BF)
    table[...] = added(tables).astype(BF)


def first_sums(pieces, tables, after):
    return pl.pallas_call(
        first_kernel,
        out_shape=(
            jax.ShapeDtypeStruct(pieces[0].shape, BF),
            jax.ShapeDtypeStruct(tables[0].shape, BF),
        ),
        in_specs=[VMEM] * 6 + [ANY],
        out_specs=(VMEM,) * 2,
        compiler_params=params(4),
        name="first_sums",
    )(*pieces, *tables, after)


def turn_kernel(total, *refs):
    tables, outs, (total_s, table_s) = refs[:4], refs[4:8], refs[8:]
    depth = total_s.shape[1]
    for xh in range(2):
        for xl in range(2):
            total_s[xh * 2 + xl] = total[:, xl * 16 : xl * 16 + 16, xh * 256 : xh * 256 + 256]
    for step, ref in enumerate(tables):
        table_s[lax.rem(lax.axis_index("y") + 4 - step, 4)] = ref[...]
    table = added(slots(table_s)).astype(BF)
    for flip, out in enumerate(outs):
        out[:depth] = total_s[place_x() ^ flip]
        out[depth:] = table


def turn(total, tables):
    depth, table = total.shape[0], tables[0].shape
    out = jax.ShapeDtypeStruct((depth + table[0], 16, 256), BF)
    return pl.pallas_call(
        turn_kernel,
        out_shape=(out,) * 4,
        in_specs=[VMEM] * 5,
        out_specs=(VMEM,) * 4,
        scratch_shapes=[pltpu.VMEM((4, depth, 16, 256), BF), pltpu.VMEM((4,) + table, BF)],
        compiler_params=params(4),
        name="turn",
    )(total, *tables)


def mix_kernel(*refs):
    pieces, (after, out, table_s) = refs[:4], refs[4:]
    depth = out.shape[0]
    for flip, ref in enumerate(pieces):
        table_s[place_x() ^ flip] = ref[depth:]
    table = added(slots(table_s)).astype(BF)
    out[:, 0] = added([ref.at[:depth] for ref in pieces]).astype(BF)
    for z in range(depth):
        out[z, 1:] = table


def mix(pieces, after):
    rows = PARTS // 2
    return pl.pallas_call(
        mix_kernel,
        out_shape=jax.ShapeDtypeStruct((pieces[0].shape[0] - rows, 1 + rows, 16, 256), BF),
        in_specs=[VMEM] * 4 + [ANY],
        out_specs=VMEM,
        scratch_shapes=[pltpu.VMEM((4, rows, 16, 256), BF)],
        compiler_params=params(4),
        name="mix",
    )(*pieces, after)


def final_kernel(pieces, out, table):
    total = added(slots(pieces))
    out[...] = total[0]
    for part in range(PARTS):
        at = part % 2 * 128
        lanes = min(128, NREL - part * 128)
        table[:, part * 128 : part * 128 + lanes] = total[1 + part // 2, :, at : at + lanes]


def final(pieces):
    return pl.pallas_call(
        final_kernel,
        out_shape=(
            jax.ShapeDtypeStruct((16, 256), F32),
            jax.ShapeDtypeStruct((HEADS, NREL), F32),
        ),
        in_specs=[VMEM],
        out_specs=(VMEM,) * 2,
        compiler_params=params(4),
        name="final",
    )(pieces)


def join_kernel(own, lon, lat, out, own_s, lon_s, lat_s, line):
    own_s[...] = own[...].astype(F32)
    lon_s[...] = lon[...].astype(F32)
    lat_s[...] = lat[...].astype(F32)
    for level, row, at in groups():
        line[:HALF_LON] = lat_s[at + PIECE : at + PIECE + HALF_LON]
        line[HALF_LON:] = lat_s[at : at + HALF_LON]
        out[level, row] = line[...].astype(BF)
        line[:HALF_LON] = lon_s[at : at + HALF_LON]
        line[HALF_LON:] = own_s[at : at + HALF_LON]
        out[level, row + HALF_LAT] = line[...].astype(BF)


def join(own, lon, lat):
    return pl.pallas_call(
        join_kernel,
        out_shape=jax.ShapeDtypeStruct((LEVELS, WLAT, WLON, D), BF),
        in_specs=[VMEM] * 3,
        out_specs=VMEM,
        scratch_shapes=[
            pltpu.VMEM((PIECE, D), F32),
            pltpu.VMEM((2 * PIECE, D), F32),
            pltpu.VMEM((2 * PIECE, D), F32),
            pltpu.VMEM((WLON, D), F32),
        ],
        compiler_params=params(4),
        name="join",
    )(own, lon, lat)


def shift(array, axes, by):
    peers = lax.axis_size(axes)
    return lax.ppermute(array, axes, [(i, (i + by) % peers) for i in range(peers)])


def shift_both(array, by):
    lats, lons = lax.axis_size(LAT), lax.axis_size(LON)
    pairs = [
        (a * lons + b, ((a + by) % lats) * lons + (b + by) % lons)
        for a in range(lats)
        for b in range(lons)
    ]
    return lax.ppermute(array, ALL, pairs)


def exchange(pieces, axes):
    return lax.all_to_all(pieces, axes, 0, 0, tiled=True)


def along_y(pieces):
    return [pieces[0]] + [shift(pieces[step], "y", step) for step in range(1, 4)]


def along_x(pieces):
    flips = [[(i, i ^ flip) for i in range(4)] for flip in range(4)]
    return [pieces[0]] + [lax.ppermute(pieces[flip], XS, flips[flip]) for flip in range(1, 4)]


def body(tokens, cotangent, qkv_weight, out_weight, bias_table, rel_index):
    swap = [(0, 1), (1, 0)]
    send = pack(tokens, cotangent)
    lon = shift(send[0], LON, -1)
    lat = shift(send[1], LAT, -1)
    dia = shift_both(send[2], -1)
    bias, packed = bias_of(bias_table.T, rel_index)
    cot, att, give, proj, probs, normed, std = forward(
        tokens, cotangent, lon, lat, dia, bias, qkv_weight
    )
    far = lax.ppermute(give, "core", swap)
    gatt = grad_att(cot, out_weight)
    pieces = outer(lax.axis_size("y"), lax.axis_size("z"), cot, att, far, gatt)
    ph, ds, grads = score_grads(gatt, probs, proj, pieces[0])
    table = table_of(grads, packed)
    own, lon, lat = backward(cot, std, qkv_weight, proj, gatt, ph, ds, normed, table)
    far = lax.ppermute(table, "core", swap)
    total, table = first_sums(along_y(pieces), (table, far), own)
    pieces = along_x(turn(total, along_y([table] * 4)))
    lon = shift(lon, LON, 1)
    parts = mix(pieces, lon)
    lat = shift(jnp.concatenate([lat, lon[PIECE:]], axis=0), LAT, 1)
    out_grad, table_grad = final(exchange(parts, "z"))
    return (join(own, lon, lat), out_grad.T, table_grad.T)


def solution(mesh):
    fine = Mesh(mesh.devices.reshape(2, 2, 8, 4, 2), ALL)
    grid = P(None, LAT, LON, None)
    return jax.shard_map(
        body,
        mesh=fine,
        in_specs=(grid, grid, P(), P(), P(), P()),
        out_specs=(grid, P(LAT, LON), P()),
        check_vma=False,
    )
```
